256 devices in a mesh: pts: 8 (over z), cent: 32 (over x, y, core).
Axes of the slice: x: 4, y: 4, z: 8, core: 2. Of those that a mesh axis runs over, the one named last changes fastest.
Arguments:
- points: bfloat16 [8192, 1024], P('pts', 'cent'), may hold values from -1 to 1, as said below
- centroids: bfloat16 [65536, 1024], P('cent'), may hold values from -1.25 to 1.25, as said below
Outputs:
- grad_points: float32 [8192, 1024], P('pts', 'cent')
- grad_centroids: float32 [65536, 1024], P('cent', 'pts')
- loss: float32 [], replicated
The draws below stay inside these ranges and needn't reach their ends.
Inputs may be any that keep to these rules, and one draw needn't show every extreme that they name: centroids are independent rows with scales spread over a range. `points`: each point lies near a scaled centroid.
All inputs are finite; a program needn't handle non-finite values.
Results may differ from the reference program's by a relative error of at most 0.0003.
Values may be sent and summed in bfloat16 or wider, within the bound.
No kernel may reach another device: no remote copies, remote signals or barrier semaphores. Data moves between devices by JAX's collectives and lax.ppermute only.
A program may use at most 256 MiB of HBM per device.

```python
import jax
import jax.numpy as jnp
from jax import lax

D = 1024
CENT_DEV = 2048
POINTS = 8192
CLUSTERS = 65536
N_CENT = 32


def centre_rows(key, low, high):
    key = jax.random.fold_in(key, 11)
    key_scale, key_base = jax.random.split(key)
    logs = jax.random.uniform(key_scale, (CLUSTERS, 1), jnp.float32, jnp.log(low), jnp.log(high))
    normal_base = jnp.clip(jax.random.normal(key_base, (CLUSTERS, D), jnp.float32), -4.0, 4.0)
    base = normal_base
    return base * jnp.exp(logs)


def draw_centroids(key, part):
    rows = centre_rows(key, 0.02, 0.3)
    return rows.astype(jnp.bfloat16)


def draw_points(key, part):
    rows = centre_rows(key, 0.02, 0.3)
    key = jax.random.fold_in(key, 13)
    key_pick, key_noise = jax.random.split(key)
    picks = jax.random.randint(key_pick, (POINTS,), 0, CLUSTERS)
    near = 0.7 * rows[picks]
    noise = 0.01 * jnp.clip(jax.random.normal(key_noise, (POINTS, D), jnp.float32), -4.0, 4.0)
    return (near + noise).astype(jnp.bfloat16)


def setup_inputs(seed: int = 0) -> dict:
    key_list = jax.random.split(jax.random.key(seed), 3)
    return {
        "points": draw_points(jax.random.fold_in(key_list[2], 71), 0),
        "centroids": draw_centroids(jax.random.fold_in(key_list[2], 71), 0),
    }


def reference(points, centroids):
    blocks = centroids.reshape(N_CENT, CENT_DEV, D)
    zf = points.astype(jnp.float32)
    zsq = jnp.sum(zf * zf, axis=1)

    def kernel_of(block):
        dots = jnp.dot(points, block.T, preferred_element_type=jnp.float32)
        bf = block.astype(jnp.float32)
        msq = jnp.sum(bf * bf, axis=1)
        return 1.0 / (1.0 + zsq[:, None] + msq[None, :] - 2.0 * dots)

    def first(carry, block):
        return carry + jnp.sum(kernel_of(block), axis=1), None

    norm, unused = lax.scan(first, jnp.zeros((POINTS,), jnp.float32), blocks)

    def sharpen(block):
        kern = kernel_of(block)
        soft = kern / norm[:, None]
        freq = jnp.sum(soft, axis=0)
        return kern, soft, soft * soft / freq[None, :]

    def second(carry, block):
        kern, soft, sharp = sharpen(block)
        return carry + jnp.sum(sharp, axis=1), None

    denom, unused = lax.scan(second, jnp.zeros((POINTS,), jnp.float32), blocks)

    def third(carry, block):
        kl_sum, gz = carry
        kern, soft, sharp = sharpen(block)
        target = sharp / denom[:, None]
        kl_sum = kl_sum + jnp.sum(target * jnp.log(target / soft))
        coef = kern * (target - soft)
        bfl = block.astype(jnp.float32)
        gz = gz + jnp.sum(coef, axis=1)[:, None] * zf - jnp.dot(coef, bfl, precision=lax.Precision.HIGHEST)
        gm = jnp.dot(coef.T, zf, precision=lax.Precision.HIGHEST) - jnp.sum(coef, axis=0)[:, None] * bfl
        return (kl_sum, gz), gm

    init = (jnp.zeros((), jnp.float32), jnp.zeros((POINTS, D), jnp.float32))
    (kl_sum, gz), gm = lax.scan(third, init, blocks)
    scale = 2.0 * CLUSTERS / POINTS
    grad_points = scale * gz
    grad_centroids = -scale * gm.reshape(CLUSTERS, D)
    return grad_points, grad_centroids, kl_sum / POINTS
```

```python
import jax
import jax.numpy as jnp
from jax import lax
from jax.sharding import PartitionSpec as P

NX, NY, NC, NZ = 4, 4, 2, 8


def cent_id(x, y, c):
    return (x * NY + y) * NC + c


def cent_shift(dx, dy, dc):
    pairs = []
    for x in range(NX):
        for y in range(NY):
            for c in range(NC):
                src = cent_id(x, y, c)
                dst = cent_id((x + dx) % NX, (y + dy) % NY, c ^ dc)
                pairs.append((src, dst))
    return pairs


def z_shift(k):
    return [(i, (i + k) % NZ) for i in range(NZ)]


def sum_over(v, axis, n):
    w = jnp.broadcast_to(v[None], (n,) + v.shape)
    return lax.all_to_all(w, axis, 0, 0).sum(0)


def gather_points(v, x, y, c):
    def stage(v, shifts):
        return jnp.stack([v] + [lax.ppermute(v, "cent", cent_shift(*d)) for d in shifts])

    v = stage(v, [(0, k, 0) for k in (1, 2, 3)])
    v = stage(v, [(k, 0, 0) for k in (1, 2, 3)])
    v = stage(v, [(0, 0, 1)])
    xs = (x - jnp.arange(NX)) % NX
    ys = (y - jnp.arange(NY)) % NY
    cs = (c + jnp.arange(NC)) % NC
    v = v[cs][:, xs][:, :, ys]
    return v.transpose(1, 2, 0, 3, 4).reshape(NX * NY * NC * v.shape[3], v.shape[4])


def scatter_points(v, x, y, c):
    def pick(v, k, axis):
        return lax.dynamic_index_in_dim(v, k, axis, keepdims=False)

    rows, cols = v.shape
    v = v.reshape(NX, NY, NC, rows // (NX * NY * NC), cols)
    v = pick(v, c, 2) + lax.ppermute(pick(v, 1 - c, 2), "cent", cent_shift(0, 0, 1))
    v = sum(
        [lax.ppermute(pick(v, (x + k) % NX, 0), "cent", cent_shift(k, 0, 0)) for k in (1, 2, 3)],
        pick(v, x, 0),
    )
    v = sum(
        [lax.ppermute(pick(v, (y + k) % NY, 0), "cent", cent_shift(0, k, 0)) for k in (1, 2, 3)],
        pick(v, y, 0),
    )
    return v


def ring(part, z):
    half = part(0).shape[0] // 2
    first = part(z + 4)
    right = lax.ppermute(first[:half], "pts", z_shift(1))
    left = lax.ppermute(first[half:], "pts", z_shift(-1))
    for k in (3, 2, 1):
        a, b = part(z + k), part(z - k)
        if k == 3:
            a = jnp.concatenate([a[:half] + right, a[half:]])
            b = jnp.concatenate([b[:half], b[half:] + left])
        else:
            a, b = a + right, b + left
        right = lax.ppermute(a, "pts", z_shift(1))
        left = lax.ppermute(b, "pts", z_shift(-1))
    return part(z) + right + left


def split(v):
    hi = v.astype(jnp.bfloat16)
    lo = (v - hi.astype(jnp.float32)).astype(jnp.bfloat16)
    return hi, lo


def dot(a, b):
    return jnp.dot(a, b, preferred_element_type=jnp.float32)


def per_device(points, centroids):
    me = lax.axis_index("cent")
    z = lax.axis_index("pts")
    x, y, c = me // (NY * NC), (me // NC) % NY, me % NC
    zt = gather_points(points.T, x, y, c)
    rows = zt.shape[1]
    total = rows * NZ
    clusters = centroids.shape[0] * NX * NY * NC
    scale = 2.0 * clusters / total
    zf = zt.astype(jnp.float32)
    zsq = jnp.sum(zf * zf, axis=0)
    cf = centroids.astype(jnp.float32)
    msq = jnp.sum(cf * cf, axis=1)
    dots = dot(centroids, zt)
    kern = 1.0 / (1.0 + zsq[None, :] + msq[:, None] - 2.0 * dots)
    norm = sum_over(jnp.sum(kern, axis=0), "cent", 32)
    soft = kern / norm[None, :]
    freq = sum_over(jnp.sum(soft, axis=1), "pts", NZ)
    ratio = soft / freq[:, None]
    sharp = soft * ratio
    both = jnp.stack([jnp.sum(sharp, axis=0), jnp.sum(sharp * jnp.log(ratio * total), axis=0)])
    denom, cross = sum_over(both, "cent", 32)
    kl = jnp.sum(cross / denom - jnp.log(denom * total))
    loss = jnp.sum(sum_over(jnp.broadcast_to(kl, (128,)), "pts", NZ)[0]) / total
    coef = kern * (sharp / denom[None, :] - soft)
    hi, lo = split(coef)
    zn = zt.T
    g = dot(hi, zn) + dot(lo, zn) - jnp.sum(coef, axis=1)[:, None] * cf

    def part(owner):
        return lax.dynamic_slice_in_dim(g, (owner % NZ) * (g.shape[1] // NZ), g.shape[1] // NZ, axis=1)

    grad_centroids = -scale * ring(part, z)
    ct = centroids.T
    p = jnp.sum(coef, axis=0)[None, :] * zf - dot(ct, hi) - dot(ct, lo)
    grad_points = scale * scatter_points(p, x, y, c).T
    return (grad_points, grad_centroids, loss)


def solution(mesh):
    in_specs = (P("pts", "cent"), P("cent", None))
    out_specs = (P("pts", "cent"), P("cent", "pts"), P())
    return jax.shard_map(per_device, mesh=mesh, in_specs=in_specs, out_specs=out_specs, check_vma=False)
```

```python
import functools

import jax
import jax.numpy as jnp
from jax import lax
from jax.experimental import pallas as pl
from jax.experimental.pallas import tpu as pltpu
from jax.sharding import PartitionSpec as P

NX, NY, NC, NZ = 4, 4, 2, 8
NCENT = NX * NY * NC
D = 1024
ROWS = 1024
CENT = 2048
TOTAL = ROWS * NZ
SCALE = 2.0 * CENT * NCENT / TOTAL
CHUNK = D // NZ
HALF = CENT // 2
PAD = 16
TILE = 256
STEPS = CENT // TILE
WIDE = 512
SLAB = 256
WSTEPS = CENT // WIDE
BLOCK = D // NCENT
LANES = 128
F32 = jnp.float32
BF16 = jnp.bfloat16
POWER, WIDTH, SHIFT = 31.0, 255.0, 125.0


def cent_id(x, y, c):
    return (x * NY + y) * NC + c


def cent_shift(dx, dy, dc):
    pairs = []
    for x in range(NX):
        for y in range(NY):
            for c in range(NC):
                pairs.append((cent_id(x, y, c), cent_id((x + dx) % NX, (y + dy) % NY, c ^ dc)))
    return pairs


def z_shift(k):
    return [(i, (i + k) % NZ) for i in range(NZ)]


def dot(a, b):
    return jnp.dot(a, b, preferred_element_type=F32)


def as_row(tile):
    return jnp.concatenate([tile[k : k + 1, :] for k in range(tile.shape[0])], axis=1)


def store_tile(ref, row, lead, first):
    for k in range(row.shape[1] // LANES):
        piece = row[:, k * LANES : (k + 1) * LANES]
        ref[:, first + k, :] = jnp.broadcast_to(piece, (lead, LANES))


def column_blocks(tile, first, count):
    cols = []
    for k in range(count):
        row = tile[first + k : first + k + 1, :]
        cols.append(jnp.transpose(jnp.broadcast_to(row, (LANES, LANES))))
    return jnp.concatenate(cols, axis=0)


def lane_wide(col, width):
    return jnp.concatenate([col] * (width // LANES), axis=1)


def lane_fold(v):
    return functools.reduce(jnp.add, [v[:, k * LANES : (k + 1) * LANES] for k in range(v.shape[1] // LANES)])


def call(body, grid, in_specs, out_specs, out_shape, scratch=(), prefetch=0, vmem=8, flops=0, nbytes=0):
    return pl.pallas_call(
        body,
        grid_spec=pltpu.PrefetchScalarGridSpec(
            num_scalar_prefetch=prefetch,
            grid=grid,
            in_specs=in_specs,
            out_specs=out_specs,
            scratch_shapes=list(scratch),
        ),
        out_shape=out_shape,
        compiler_params=pltpu.CompilerParams(
            dimension_semantics=("arbitrary",) * len(grid), vmem_limit_bytes=vmem << 20
        ),
        cost_estimate=pl.CostEstimate(flops=flops, bytes_accessed=nbytes, transcendentals=0),
    )


def in_hbm(v):
    return pltpu.with_memory_space_constraint(v, pltpu.HBM)


def whole(shape):
    return pl.BlockSpec(shape, lambda *_: (0,) * len(shape))


def shaped(shape, dtype=F32):
    return jax.ShapeDtypeStruct(shape, dtype)


def kern_body(at, mine, other, cent, kern, norm, zt, zn, zsq, acc, sems):
    step = pl.program_id(0)

    @pl.when(step == 0)
    def _():
        copies = []
        for cr in range(NC):
            src = (mine, other)[cr]
            for xr in range(NX):
                for yr in range(NY):
                    xx = lax.rem(at[0] + NX - xr, NX)
                    yy = lax.rem(at[1] + NY - yr, NY)
                    cc = lax.rem(at[2] + cr, NC)
                    row = pl.multiple_of(((xx * NY + yy) * NC + cc) * BLOCK, BLOCK)
                    copies.append(
                        pltpu.make_async_copy(
                            src.at[xr, yr], zt.at[pl.ds(row, BLOCK), :], sems.at[(cr * NX + xr) * NY + yr]
                        )
                    )
        for cp in copies:
            cp.start()
        for cp in copies:
            cp.wait()
        total = jnp.zeros((8, ROWS), F32)
        for k in range(D // LANES):
            v = zt[k * LANES : (k + 1) * LANES, :].astype(F32)
            v = v * v
            total = total + jnp.sum(v.reshape(LANES // 8, 8, ROWS), axis=0)
        zsq[...] = 1.0 + jnp.sum(total, axis=0, keepdims=True)
        acc[...] = jnp.zeros_like(acc)

    c = cent[...]
    cf = c.astype(F32)
    msq = jnp.sum(lane_fold(cf * cf), axis=1, keepdims=True)
    for k in range(ROWS // SLAB):
        cols = slice(k * SLAB, (k + 1) * SLAB)
        dots = dot(c, zt[:, cols])
        v = 1.0 / ((zsq[:, cols] + msq) - 2.0 * dots)
        kern[:, cols] = v
        acc[:, cols] += jnp.sum(v.reshape(WIDE // 8, 8, SLAB), axis=0)
    part = D // WSTEPS
    first = pl.multiple_of(step * part, part)
    zn[:, pl.ds(first, part)] = jnp.transpose(zt[pl.ds(first, part), :])

    @pl.when(step == WSTEPS - 1)
    def _():
        store_tile(norm, jnp.sum(acc[...], axis=0, keepdims=True), NCENT, 0)


def kern_call(at, mine, other, centroids):
    return call(
        kern_body,
        (WSTEPS,),
        [
            pl.BlockSpec(memory_space=pl.ANY),
            pl.BlockSpec(memory_space=pl.ANY),
            pl.BlockSpec((WIDE, D), lambda s, *_: (s, 0)),
        ],
        [
            pl.BlockSpec((WIDE, ROWS), lambda s, *_: (s, 0)),
            whole((NCENT, 8, LANES)),
            whole((D, ROWS)),
            whole((ROWS, D)),
        ],
        [shaped((CENT, ROWS)), shaped((NCENT, 8, LANES)), shaped((D, ROWS), BF16), shaped((ROWS, D), BF16)],
        [pltpu.VMEM((1, ROWS), F32), pltpu.VMEM((8, ROWS), F32), pltpu.SemaphoreType.DMA((NCENT,))],
        prefetch=1,
        vmem=14,
        flops=2 * CENT * ROWS * D,
        nbytes=20 << 20,
    )(at, mine, other, in_hbm(centroids))


def freq_body(norms, kern, freq, inv, row):
    step = pl.program_id(0)

    @pl.when(step == 0)
    def _():
        tile = 1.0 / jnp.sum(norms[...], axis=0)
        inv[...] = tile
        row[...] = as_row(tile)

    part = lane_fold(kern[...] * row[...])
    for k in range(TILE // LANES):
        block = jnp.transpose(part[k * LANES : (k + 1) * LANES, :])
        line = jnp.sum(block, axis=0, keepdims=True)
        freq[:, pl.ds(step * (TILE // LANES) + k, 1), :] = jnp.broadcast_to(line[None], (NZ, 1, LANES))


def freq_call(norms, kern):
    return call(
        freq_body,
        (STEPS,),
        [whole((NCENT, 8, LANES)), pl.BlockSpec((TILE, ROWS), lambda s: (s, 0))],
        [whole((NZ, CENT // LANES, LANES)), whole((8, LANES))],
        [shaped((NZ, CENT // LANES, LANES)), shaped((8, LANES))],
        [pltpu.VMEM((1, ROWS), F32)],
        vmem=6,
        flops=CENT * ROWS * 2,
        nbytes=8 << 20,
    )(norms, kern)


def frequency_columns(rf, step):
    tile = rf[pl.ds(pl.multiple_of(step * (TILE // LANES), TILE // LANES), TILE // LANES), :]
    return lane_wide(column_blocks(tile, 0, TILE // LANES), ROWS)


def denom_body(freqs, inv, kern, out, rf, row, dsum, csum):
    step = pl.program_id(0)

    @pl.when(step == 0)
    def _():
        rf[...] = 1.0 / jnp.sum(freqs[...], axis=0)
        row[...] = as_row(inv[...])
        dsum[...] = jnp.zeros_like(dsum)
        csum[...] = jnp.zeros_like(csum)

    soft = kern[...] * row[...]
    ratio = soft * frequency_columns(rf, step)
    sharp = soft * ratio
    dsum[...] += jnp.sum(sharp.reshape(TILE // 8, 8, ROWS), axis=0)
    csum[...] += jnp.sum((sharp * jnp.log(ratio * float(TOTAL))).reshape(TILE // 8, 8, ROWS), axis=0)

    @pl.when(step == STEPS - 1)
    def _():
        store_tile(out, jnp.sum(dsum[...], axis=0, keepdims=True), NCENT, 0)
        store_tile(out, jnp.sum(csum[...], axis=0, keepdims=True), NCENT, 8)


def denom_call(freqs, inv, kern):
    return call(
        denom_body,
        (STEPS,),
        [
            whole((NZ, CENT // LANES, LANES)),
            whole((8, LANES)),
            pl.BlockSpec((TILE, ROWS), lambda s: (s, 0)),
        ],
        whole((NCENT, 16, LANES)),
        shaped((NCENT, 16, LANES)),
        [
            pltpu.VMEM((CENT // LANES, LANES), F32),
            pltpu.VMEM((1, ROWS), F32),
            pltpu.VMEM((8, ROWS), F32),
            pltpu.VMEM((8, ROWS), F32),
        ],
        vmem=8,
        flops=CENT * ROWS * 6,
        nbytes=8 << 20,
    )(freqs, inv, kern)


def exponent(v):
    size = jnp.abs(v)
    top = jnp.maximum(jnp.max(jnp.max(size, axis=0, keepdims=True), axis=1, keepdims=True), 1e-30)
    return jnp.ceil(jnp.log2(top))


def code(v, expo):
    unit = jnp.minimum(jnp.abs(v) * jnp.exp2(-expo), 1.0)
    c = jnp.exp2(POWER * jnp.log2(1.0 + WIDTH * unit) - SHIFT)
    return jnp.where(v < 0.0, -c, c).astype(BF16)


def uncode(c, expo):
    c = c.astype(F32)
    unit = (jnp.exp2((jnp.log2(jnp.abs(c)) + SHIFT) * (1.0 / POWER)) - 1.0) * (1.0 / WIDTH)
    unit = unit * jnp.exp2(expo)
    return jnp.where(c < 0.0, -unit, unit)


def encode(v, slots, msg):
    rows = v.shape[0]
    expo = exponent(v)
    msg[:rows, :] = code(v, expo)
    high = slots.astype(BF16).astype(F32)
    mid = (slots - high).astype(BF16).astype(F32)
    low = slots - high - mid
    tail = [jnp.broadcast_to(expo, (1, v.shape[1])), high, mid, low, jnp.zeros((PAD - 4, v.shape[1]), F32)]
    msg[rows:, :] = jnp.concatenate(tail, axis=0).astype(BF16)


def decode(msg):
    rows = msg.shape[0] - PAD
    tail = msg[rows:, :].astype(F32)
    return uncode(msg[:rows, :], tail[0:1, :]), (tail[1:2, :] + tail[2:3, :]) + tail[3:4, :]


MSG = (CENT + PAD, CHUNK)
FIRST = (HALF + PAD, CHUNK)


def coef_body(z, dens, freqs, inv, kern, cent, zn, hi, lo, csum, kl, g, right, left, rf, row, rden, first):
    step = pl.program_id(0)

    @pl.when(step == 0)
    def _():
        rf[...] = 1.0 / jnp.sum(freqs[...], axis=0)
        row[...] = as_row(inv[...])
        both = jnp.sum(dens[...], axis=0)
        rtile = 1.0 / both[:8]
        rden[...] = as_row(rtile)
        part = both[8:] * rtile - jnp.log(both[:8] * float(TOTAL))
        part = jnp.sum(jnp.sum(part, axis=0, keepdims=True), axis=1, keepdims=True) * (1.0 / TOTAL)
        lane = lax.broadcasted_iota(jnp.int32, kl.shape, 1)
        kl[...] = jnp.where(lane == z[0], jnp.broadcast_to(part, kl.shape), 0.0)
        csum[...] = jnp.zeros_like(csum)

    far = lax.rem(z[0] + NZ // 2, NZ)
    total = jnp.zeros((8, ROWS), F32)
    for sub in range(WIDE // TILE):
        at = slice(sub * TILE, (sub + 1) * TILE)
        k = kern[at, :]
        soft = k * row[...]
        fc = frequency_columns(rf, step * (WIDE // TILE) + sub)
        coef = k * (soft * soft * fc * rden[...] - soft)
        h = coef.astype(BF16)
        l = (coef - h.astype(F32)).astype(BF16)
        hi[at, :] = h
        lo[at, :] = l
        total = total + jnp.sum(coef.reshape(TILE // 8, 8, ROWS), axis=0)
        e = jnp.sum(lane_fold(coef), axis=1, keepdims=True)
        both = jnp.concatenate([h, l], axis=0)
        for n in range(D // SLAB):
            cols = slice(n * SLAB, (n + 1) * SLAB)
            r = dot(both, zn[:, cols])
            r = r[:TILE] + r[TILE:] - e * cent[at, cols].astype(F32)
            for o in range(SLAB // CHUNK):
                g[n * (SLAB // CHUNK) + o, at, :] = r[:, o * CHUNK : (o + 1) * CHUNK]
    csum[...] += total
    first[pl.ds(pl.multiple_of(step * WIDE, WIDE), WIDE), :] = g[pl.ds(far, 1)][0]

    @pl.when(step == WSTEPS - 1)
    def _():
        encode(first[:HALF, :], kl[0:1, :], right)
        encode(first[HALF:, :], jnp.zeros((1, LANES), F32), left)


def coef_call(z, dens, freqs, inv, kern, centroids, zn):
    tiles = pl.BlockSpec((WIDE, ROWS), lambda s, z: (s, 0))
    return call(
        coef_body,
        (WSTEPS,),
        [
            whole((NCENT, 16, LANES)),
            whole((NZ, CENT // LANES, LANES)),
            whole((8, LANES)),
            tiles,
            pl.BlockSpec((WIDE, D), lambda s, z: (s, 0)),
            whole((ROWS, D)),
        ],
        [
            tiles,
            tiles,
            whole((8, ROWS)),
            whole((8, LANES)),
            pl.BlockSpec((NZ, WIDE, CHUNK), lambda s, z: (0, s, 0)),
            whole(FIRST),
            whole(FIRST),
        ],
        [
            shaped((CENT, ROWS), BF16),
            shaped((CENT, ROWS), BF16),
            shaped((8, ROWS)),
            shaped((8, LANES)),
            shaped((NZ, CENT, CHUNK)),
            shaped(FIRST, BF16),
            shaped(FIRST, BF16),
        ],
        [
            pltpu.VMEM((CENT // LANES, LANES), F32),
            pltpu.VMEM((1, ROWS), F32),
            pltpu.VMEM((1, ROWS), F32),
            pltpu.VMEM((CENT, CHUNK), F32),
        ],
        prefetch=1,
        vmem=18,
        flops=4 * CENT * ROWS * D,
        nbytes=30 << 20,
    )(z, dens, freqs, inv, kern, in_hbm(centroids), zn)


def hop_body(k, at, a, b, kl, got_right, got_left, right, left):
    for part, got, msg, first in ((a, got_right, right, 0), (b, got_left, left, HALF)):
        v, slots = decode(got)
        full = part[0]
        if k == NZ // 2 - 1:
            own = full[first : first + HALF, :] + v
            rest = full[HALF - first : CENT - first, :]
            full = jnp.concatenate([own, rest] if first == 0 else [rest, own], axis=0)
        else:
            full = full + v
        encode(full, slots + kl[0:1, :], msg)


def part_spec(k):
    return pl.BlockSpec((1, CENT, CHUNK), lambda s, z: (lax.rem(z[0] + k + NZ, NZ), 0, 0))


def hop_call(z, g, kl, k, got):
    return call(
        functools.partial(hop_body, k),
        (1,),
        [part_spec(k), part_spec(-k), whole((8, LANES)), whole(got[0].shape), whole(got[1].shape)],
        [whole(MSG), whole(MSG)],
        [shaped(MSG, BF16)] * 2,
        prefetch=1,
        vmem=14,
        flops=4 * CENT * CHUNK * 40,
        nbytes=3 << 20,
    )(z, g, g, kl, *got)


def end_body(at, own, kl, right, left, out, loss):
    (r, before), (l, after) = decode(right), decode(left)
    out[...] = (own[0] + r + l) * -SCALE
    total = jnp.sum(kl[0:1, :] + before + after, axis=1, keepdims=True)
    loss[...] = jnp.broadcast_to(total, loss.shape)


def end_call(z, g, kl, right, left):
    return call(
        end_body,
        (1,),
        [part_spec(0), whole((8, LANES)), whole(MSG), whole(MSG)],
        [whole((CENT, CHUNK)), whole((8, LANES))],
        [shaped((CENT, CHUNK)), shaped((8, LANES))],
        prefetch=1,
        vmem=10,
        flops=4 * CENT * CHUNK * 20,
        nbytes=4 << 20,
    )(z, g, kl, right, left)


def point_body(cent, hi, lo, csum, zt, out):
    c = cent[...]
    dims = (((0,), (0,)), ((), ()))
    g = lax.dot_general(c, hi[...], dims, preferred_element_type=F32)
    g = g + lax.dot_general(c, lo[...], dims, preferred_element_type=F32)
    total = jnp.sum(csum[...], axis=0, keepdims=True)
    v = total * zt[...].astype(F32) - g
    expo = exponent(v)
    for k in range(TILE // BLOCK):
        out[k, :, :ROWS] = code(v[k * BLOCK : (k + 1) * BLOCK, :], expo)
        out[k, :, ROWS:] = jnp.broadcast_to(expo, (BLOCK, LANES)).astype(BF16)


def point_call(centroids, hi, lo, csum, zt):
    block = (TILE // BLOCK, BLOCK, ROWS + LANES)
    return call(
        point_body,
        (D // TILE,),
        [
            pl.BlockSpec((CENT, TILE), lambda s: (0, s)),
            whole((CENT, ROWS)),
            whole((CENT, ROWS)),
            whole((8, ROWS)),
            pl.BlockSpec((TILE, ROWS), lambda s: (s, 0)),
        ],
        pl.BlockSpec(block, lambda s: (s, 0, 0)),
        shaped((NCENT, BLOCK, ROWS + LANES), BF16),
        vmem=18,
        flops=4 * CENT * ROWS * D,
        nbytes=18 << 20,
    )(in_hbm(centroids), hi, lo, csum, zt)


def point_sum_body(msgs, out):
    total = jnp.zeros(out.shape, F32)
    for k in range(NCENT):
        total = total + uncode(msgs[k, :, :ROWS], msgs[k, 0:1, ROWS : ROWS + 1].astype(F32))
    out[...] = total * SCALE


def point_sum_call(msgs):
    return call(
        point_sum_body,
        (1,),
        [whole(msgs.shape)],
        whole((BLOCK, ROWS)),
        shaped((BLOCK, ROWS)),
        vmem=10,
        flops=D * ROWS * 20,
        nbytes=3 << 20,
    )(msgs)


def gather_points(v):
    def stage(v, shifts):
        return jnp.stack([v] + [lax.ppermute(v, "cent", cent_shift(*d)) for d in shifts])

    v = stage(v, [(0, k, 0) for k in (1, 2, 3)])
    v = stage(v, [(k, 0, 0) for k in (1, 2, 3)])
    return v, lax.ppermute(v, "cent", cent_shift(0, 0, 1))


def per_device(points, centroids):
    me = lax.axis_index("cent")
    x, y, c = me // (NY * NC), (me // NC) % NY, me % NC
    at = jnp.stack([x, y, c]).astype(jnp.int32)
    zi = lax.axis_index("pts").astype(jnp.int32)
    z = zi[None]
    mine, other = gather_points(points.T)
    kern, norm, zt, zn = kern_call(at, mine, other, centroids)
    norms = lax.all_to_all(norm, "cent", 0, 0)
    freq, inv = freq_call(norms, kern)
    freqs = lax.all_to_all(freq, "pts", 0, 0)
    den = denom_call(freqs, inv, kern)
    dens = lax.all_to_all(den, "cent", 0, 0)
    hi, lo, csum, kl, g, ra, la = coef_call(z, dens, freqs, inv, kern, centroids, zn)

    def send(right, left):
        return lax.ppermute(right, "pts", z_shift(1)), lax.ppermute(left, "pts", z_shift(-1))

    got = send(ra, la)
    msgs = hop_call(z, g, kl, 3, got)
    hi, lo, right, left = lax.optimization_barrier((hi, lo, *msgs))
    got = send(right, left)
    pmsgs = point_call(centroids, hi, lo, csum, zt)
    pmsgs, right, left = lax.optimization_barrier((pmsgs, *got))
    got = (right, left)
    for k in (2, 1):
        got = send(*hop_call(z, g, kl, k, got))
    grad_centroids, loss = end_call(z, g, kl, *got)
    grad_points = point_sum_call(lax.all_to_all(pmsgs, "cent", 0, 0)).T
    return (grad_points, grad_centroids, loss[0, 0])


def solution(mesh):
    in_specs = (P("pts", "cent"), P("cent", None))
    out_specs = (P("pts", "cent"), P("cent", "pts"), P())
    return jax.shard_map(per_device, mesh=mesh, in_specs=in_specs, out_specs=out_specs, check_vma=False)
```

```python
import functools

import jax
import jax.numpy as jnp
from jax import lax
from jax.experimental import pallas as pl
from jax.experimental.pallas import tpu as pltpu
from jax.sharding import PartitionSpec as P

NX, NY, NC, NZ = 4, 4, 2, 8
NCENT = NX * NY * NC
D = 1024
ROWS = 1024
CENT = 2048
TOTAL = ROWS * NZ
SCALE = 2.0 * CENT * NCENT / TOTAL
CHUNK = D // NZ
HALF = CENT // 2
PAD = 16
TILE = 256
STEPS = CENT // TILE
WIDE = 512
SLAB = 256
WSTEPS = CENT // WIDE
BLOCK = D // NCENT
LANES = 128
F32 = jnp.float32
BF16 = jnp.bfloat16
POWER, WIDTH, SHIFT = 31.0, 255.0, 125.0


def cent_id(x, y, c):
    return (x * NY + y) * NC + c


def cent_shift(dx, dy, dc):
    pairs = []
    for x in range(NX):
        for y in range(NY):
            for c in range(NC):
                pairs.append((cent_id(x, y, c), cent_id((x + dx) % NX, (y + dy) % NY, c ^ dc)))
    return pairs


def z_shift(k):
    return [(i, (i + k) % NZ) for i in range(NZ)]


def dot(a, b):
    return jnp.dot(a, b, preferred_element_type=F32)


def as_row(tile):
    return jnp.concatenate([tile[k : k + 1, :] for k in range(tile.shape[0])], axis=1)


def store_tile(ref, row, lead, first):
    for k in range(row.shape[1] // LANES):
        piece = row[:, k * LANES : (k + 1) * LANES]
        ref[:, first + k, :] = jnp.broadcast_to(piece, (lead, LANES))


def column_blocks(tile, first, count):
    cols = []
    for k in range(count):
        row = tile[first + k : first + k + 1, :]
        cols.append(jnp.transpose(jnp.broadcast_to(row, (LANES, LANES))))
    return jnp.concatenate(cols, axis=0)


def lane_wide(col, width):
    return jnp.concatenate([col] * (width // LANES), axis=1)


def lane_fold(v):
    return functools.reduce(jnp.add, [v[:, k * LANES : (k + 1) * LANES] for k in range(v.shape[1] // LANES)])


def call(body, grid, in_specs, out_specs, out_shape, scratch=(), prefetch=0, vmem=8, flops=0, nbytes=0):
    return pl.pallas_call(
        body,
        grid_spec=pltpu.PrefetchScalarGridSpec(
            num_scalar_prefetch=prefetch,
            grid=grid,
            in_specs=in_specs,
            out_specs=out_specs,
            scratch_shapes=list(scratch),
        ),
        out_shape=out_shape,
        compiler_params=pltpu.CompilerParams(
            dimension_semantics=("arbitrary",) * len(grid), vmem_limit_bytes=vmem << 20
        ),
        cost_estimate=pl.CostEstimate(flops=flops, bytes_accessed=nbytes, transcendentals=0),
    )


def in_hbm(v):
    return pltpu.with_memory_space_constraint(v, pltpu.HBM)


def whole(shape):
    return pl.BlockSpec(shape, lambda *_: (0,) * len(shape))


def shaped(shape, dtype=F32):
    return jax.ShapeDtypeStruct(shape, dtype)


def kern_body(at, mine, other, cent, kern, norm, zt_out, zn_out, zt, zn, zsq, acc, sems, osems):
    step = pl.program_id(0)
    copies = []
    for cr in range(NC):
        src = (mine, other)[cr]
        for xr in range(NX):
            for yr in range(NY):
                xx = lax.rem(at[0] + NX - xr, NX)
                yy = lax.rem(at[1] + NY - yr, NY)
                cc = lax.rem(at[2] + cr, NC)
                row = pl.multiple_of(((xx * NY + yy) * NC + cc) * BLOCK, BLOCK)
                copies.append(
                    pltpu.make_async_copy(
                        src.at[xr, yr], zt.at[pl.ds(row, BLOCK), :], sems.at[(cr * NX + xr) * NY + yr]
                    )
                )

    @pl.when(step == 0)
    def _():
        for cp in copies:
            cp.start()

    c = cent[...]
    cf = c.astype(F32)
    msq = jnp.sum(lane_fold(cf * cf), axis=1, keepdims=True)
    part = D // WSTEPS
    outs = [pltpu.make_async_copy(zt, zt_out, osems.at[WSTEPS])]
    for t in range(WSTEPS):
        cols = pl.ds(t * part, part)
        outs.append(pltpu.make_async_copy(zn.at[:, cols], zn_out.at[:, cols], osems.at[t]))

    @pl.when(step == 0)
    def _():
        for cp in copies:
            cp.wait()
        outs[0].start()
        total = jnp.zeros((8, ROWS), F32)
        for k in range(D // LANES):
            v = zt[k * LANES : (k + 1) * LANES, :].astype(F32)
            v = v * v
            total = total + jnp.sum(v.reshape(LANES // 8, 8, ROWS), axis=0)
        zsq[...] = 1.0 + jnp.sum(total, axis=0, keepdims=True)
        acc[...] = jnp.zeros_like(acc)

    for k in range(ROWS // SLAB):
        cols = slice(k * SLAB, (k + 1) * SLAB)
        dots = dot(c, zt[:, cols])
        v = 1.0 / ((zsq[:, cols] + msq) - 2.0 * dots)
        kern[:, cols] = v
        acc[:, cols] += jnp.sum(v.reshape(WIDE // 8, 8, SLAB), axis=0)
    for t in range(WSTEPS):

        @pl.when(step == t)
        def _(t=t):
            zn[:, t * part : (t + 1) * part] = jnp.transpose(zt[t * part : (t + 1) * part, :])
            outs[1 + t].start()

    @pl.when(step == WSTEPS - 1)
    def _():
        store_tile(norm, jnp.sum(acc[...], axis=0, keepdims=True), NCENT, 0)
        for cp in outs:
            cp.wait()


def kern_call(at, mine, other, centroids):
    hbm = pl.BlockSpec(memory_space=pl.ANY)
    return call(
        kern_body,
        (WSTEPS,),
        [hbm, hbm, pl.BlockSpec((WIDE, D), lambda s, *_: (s, 0))],
        [pl.BlockSpec((WIDE, ROWS), lambda s, *_: (s, 0)), whole((NCENT, 8, LANES)), hbm, hbm],
        [
            shaped((CENT, ROWS)),
            shaped((NCENT, 8, LANES)),
            pltpu.HBM((D, ROWS), BF16),
            pltpu.HBM((ROWS, D), BF16),
        ],
        [
            pltpu.VMEM((D, ROWS), BF16),
            pltpu.VMEM((ROWS, D), BF16),
            pltpu.VMEM((1, ROWS), F32),
            pltpu.VMEM((8, ROWS), F32),
            pltpu.SemaphoreType.DMA((NCENT,)),
            pltpu.SemaphoreType.DMA((WSTEPS + 1,)),
        ],
        prefetch=1,
        vmem=18,
        flops=2 * CENT * ROWS * D,
        nbytes=20 << 20,
    )(at, mine, in_hbm(other), in_hbm(centroids))


def freq_body(norms, kern, freq, inv, row):
    step = pl.program_id(0)

    @pl.when(step == 0)
    def _():
        tile = 1.0 / jnp.sum(norms[...], axis=0)
        inv[...] = tile
        row[...] = as_row(tile)

    part = lane_fold(kern[...] * row[...])
    for k in range(TILE // LANES):
        block = jnp.transpose(part[k * LANES : (k + 1) * LANES, :])
        line = jnp.sum(block, axis=0, keepdims=True)
        freq[:, pl.ds(step * (TILE // LANES) + k, 1), :] = jnp.broadcast_to(line[None], (NZ, 1, LANES))


def freq_call(norms, kern):
    return call(
        freq_body,
        (STEPS,),
        [whole((NCENT, 8, LANES)), pl.BlockSpec((TILE, ROWS), lambda s: (s, 0))],
        [whole((NZ, CENT // LANES, LANES)), whole((8, LANES))],
        [shaped((NZ, CENT // LANES, LANES)), shaped((8, LANES))],
        [pltpu.VMEM((1, ROWS), F32)],
        vmem=6,
        flops=CENT * ROWS * 2,
        nbytes=8 << 20,
    )(norms, kern)


def frequency_columns(rf, step):
    tile = rf[pl.ds(pl.multiple_of(step * (TILE // LANES), TILE // LANES), TILE // LANES), :]
    return lane_wide(column_blocks(tile, 0, TILE // LANES), ROWS)


def denom_body(freqs, inv, kern, out, rf, row, dsum, csum):
    step = pl.program_id(0)

    @pl.when(step == 0)
    def _():
        rf[...] = 1.0 / jnp.sum(freqs[...], axis=0)
        row[...] = as_row(inv[...])
        dsum[...] = jnp.zeros_like(dsum)
        csum[...] = jnp.zeros_like(csum)

    soft = kern[...] * row[...]
    ratio = soft * frequency_columns(rf, step)
    sharp = soft * ratio
    dsum[...] += jnp.sum(sharp.reshape(TILE // 8, 8, ROWS), axis=0)
    csum[...] += jnp.sum((sharp * jnp.log(ratio * float(TOTAL))).reshape(TILE // 8, 8, ROWS), axis=0)

    @pl.when(step == STEPS - 1)
    def _():
        store_tile(out, jnp.sum(dsum[...], axis=0, keepdims=True), NCENT, 0)
        store_tile(out, jnp.sum(csum[...], axis=0, keepdims=True), NCENT, 8)


def denom_call(freqs, inv, kern):
    return call(
        denom_body,
        (STEPS,),
        [
            whole((NZ, CENT // LANES, LANES)),
            whole((8, LANES)),
            pl.BlockSpec((TILE, ROWS), lambda s: (s, 0)),
        ],
        whole((NCENT, 16, LANES)),
        shaped((NCENT, 16, LANES)),
        [
            pltpu.VMEM((CENT // LANES, LANES), F32),
            pltpu.VMEM((1, ROWS), F32),
            pltpu.VMEM((8, ROWS), F32),
            pltpu.VMEM((8, ROWS), F32),
        ],
        vmem=8,
        flops=CENT * ROWS * 6,
        nbytes=8 << 20,
    )(freqs, inv, kern)


def exponent(v):
    size = jnp.abs(v)
    top = jnp.maximum(jnp.max(jnp.max(size, axis=0, keepdims=True), axis=1, keepdims=True), 1e-30)
    return jnp.ceil(jnp.log2(top))


def code(v, expo):
    unit = jnp.minimum(jnp.abs(v) * jnp.exp2(-expo), 1.0)
    c = jnp.exp2(POWER * jnp.log2(1.0 + WIDTH * unit) - SHIFT)
    return jnp.where(v < 0.0, -c, c).astype(BF16)


def uncode(c, expo):
    c = c.astype(F32)
    unit = (jnp.exp2((jnp.log2(jnp.abs(c)) + SHIFT) * (1.0 / POWER)) - 1.0) * (1.0 / WIDTH)
    unit = unit * jnp.exp2(expo)
    return jnp.where(c < 0.0, -unit, unit)


def encode(v, slots, msg):
    rows = v.shape[0]
    expo = exponent(v)
    msg[:rows, :] = code(v, expo)
    high = slots.astype(BF16).astype(F32)
    mid = (slots - high).astype(BF16).astype(F32)
    low = slots - high - mid
    tail = [jnp.broadcast_to(expo, (1, v.shape[1])), high, mid, low, jnp.zeros((PAD - 4, v.shape[1]), F32)]
    msg[rows:, :] = jnp.concatenate(tail, axis=0).astype(BF16)


def decode(msg):
    rows = msg.shape[0] - PAD
    tail = msg[rows:, :].astype(F32)
    return uncode(msg[:rows, :], tail[0:1, :]), (tail[1:2, :] + tail[2:3, :]) + tail[3:4, :]


MSG = (CENT + PAD, CHUNK)
FIRST = (HALF + PAD, CHUNK)


def coef_body(z, dens, freqs, inv, kern, cent, zn_hbm, hi, lo, csum, kl, g, right, left, rf, row, rden, first, zn, sem):
    step = pl.program_id(0)
    rows = [pl.ds(q * (ROWS // 4), ROWS // 4) for q in range(4)]
    loads = [pltpu.make_async_copy(zn_hbm.at[r], zn.at[r], sem.at[q]) for q, r in enumerate(rows)]

    @pl.when(step == 0)
    def _():
        for cp in loads:
            cp.start()
        rf[...] = 1.0 / jnp.sum(freqs[...], axis=0)
        row[...] = as_row(inv[...])
        both = jnp.sum(dens[...], axis=0)
        rtile = 1.0 / both[:8]
        rden[...] = as_row(rtile)
        part = both[8:] * rtile - jnp.log(both[:8] * float(TOTAL))
        part = jnp.sum(jnp.sum(part, axis=0, keepdims=True), axis=1, keepdims=True) * (1.0 / TOTAL)
        lane = lax.broadcasted_iota(jnp.int32, kl.shape, 1)
        kl[...] = jnp.where(lane == z[0], jnp.broadcast_to(part, kl.shape), 0.0)
        csum[...] = jnp.zeros_like(csum)

    far = lax.rem(z[0] + NZ // 2, NZ)
    total = jnp.zeros((8, ROWS), F32)
    for sub in range(WIDE // TILE):
        at = slice(sub * TILE, (sub + 1) * TILE)
        k = kern[at, :]
        soft = k * row[...]
        fc = frequency_columns(rf, step * (WIDE // TILE) + sub)
        coef = k * (soft * soft * fc * rden[...] - soft)
        h = coef.astype(BF16)
        l = (coef - h.astype(F32)).astype(BF16)
        hi[at, :] = h
        lo[at, :] = l
        total = total + jnp.sum(coef.reshape(TILE // 8, 8, ROWS), axis=0)
        e = jnp.sum(lane_fold(coef), axis=1, keepdims=True)
        both = jnp.concatenate([h, l], axis=0)
        if sub == 0:

            @pl.when(step == 0)
            def _():
                for cp in loads:
                    cp.wait()

        for n in range(D // SLAB):
            cols = slice(n * SLAB, (n + 1) * SLAB)
            r = dot(both, zn[:, cols])
            r = r[:TILE] + r[TILE:] - e * cent[at, cols].astype(F32)
            for o in range(SLAB // CHUNK):
                g[n * (SLAB // CHUNK) + o, at, :] = r[:, o * CHUNK : (o + 1) * CHUNK]
    csum[...] += total
    first[pl.ds(pl.multiple_of(step * WIDE, WIDE), WIDE), :] = g[pl.ds(far, 1)][0]

    @pl.when(step == WSTEPS - 1)
    def _():
        encode(first[:HALF, :], kl[0:1, :], right)
        encode(first[HALF:, :], jnp.zeros((1, LANES), F32), left)


def coef_call(z, dens, freqs, inv, kern, centroids, zn):
    tiles = pl.BlockSpec((WIDE, ROWS), lambda s, z: (s, 0))
    return call(
        coef_body,
        (WSTEPS,),
        [
            whole((NCENT, 16, LANES)),
            whole((NZ, CENT // LANES, LANES)),
            whole((8, LANES)),
            tiles,
            pl.BlockSpec((WIDE, D), lambda s, z: (s, 0)),
            pl.BlockSpec(memory_space=pl.ANY),
        ],
        [
            tiles,
            tiles,
            whole((8, ROWS)),
            whole((8, LANES)),
            pl.BlockSpec((NZ, WIDE, CHUNK), lambda s, z: (0, s, 0)),
            whole(FIRST),
            whole(FIRST),
        ],
        [
            shaped((CENT, ROWS), BF16),
            shaped((CENT, ROWS), BF16),
            shaped((8, ROWS)),
            shaped((8, LANES)),
            pltpu.HBM((NZ, CENT, CHUNK), F32),
            shaped(FIRST, BF16),
            shaped(FIRST, BF16),
        ],
        [
            pltpu.VMEM((CENT // LANES, LANES), F32),
            pltpu.VMEM((1, ROWS), F32),
            pltpu.VMEM((1, ROWS), F32),
            pltpu.VMEM((CENT, CHUNK), F32),
            pltpu.VMEM((ROWS, D), BF16),
            pltpu.SemaphoreType.DMA((4,)),
        ],
        prefetch=1,
        vmem=18,
        flops=4 * CENT * ROWS * D,
        nbytes=30 << 20,
    )(z, dens, freqs, inv, in_hbm(kern), in_hbm(centroids), zn)


PIECES = 4


def chunk_loads(z, g, k, part, sems):
    chunk = lax.rem(z[0] + k + NZ, NZ)
    rows = [pl.ds(q * (CENT // PIECES), CENT // PIECES) for q in range(PIECES)]
    return [pltpu.make_async_copy(g.at[chunk, r], part.at[r], sems.at[q]) for q, r in enumerate(rows)]


def hop_body(k, z, g, kl, got_right, got_left, right, left, ahead, behind, sems):
    loads = [chunk_loads(z, g, (k, -k)[i], (ahead, behind)[i], sems.at[i]) for i in range(2)]
    for cp in loads[0] + loads[1]:
        cp.start()
    sums = [decode(got_right), decode(got_left)]
    for cp in loads[0] + loads[1]:
        cp.wait()
    for (v, slots), msg, part, first in zip(sums, (right, left), (ahead, behind), (0, HALF)):
        if k == NZ // 2 - 1:
            own = part[first : first + HALF, :] + v
            rest = part[HALF - first : CENT - first, :]
            full = jnp.concatenate([own, rest] if first == 0 else [rest, own], axis=0)
        else:
            full = part[...] + v
        encode(full, slots + kl[0:1, :], msg)


def hop_call(z, g, kl, k, got):
    return call(
        functools.partial(hop_body, k),
        (1,),
        [pl.BlockSpec(memory_space=pl.ANY), whole((8, LANES)), whole(got[0].shape), whole(got[1].shape)],
        [whole(MSG), whole(MSG)],
        [shaped(MSG, BF16)] * 2,
        [
            pltpu.VMEM((CENT, CHUNK), F32),
            pltpu.VMEM((CENT, CHUNK), F32),
            pltpu.SemaphoreType.DMA((2, PIECES)),
        ],
        prefetch=1,
        vmem=14,
        flops=4 * CENT * CHUNK * 40,
        nbytes=3 << 20,
    )(z, in_hbm(g), kl, *got)


def end_body(z, g, kl, right, left, out, loss, own, sems):
    loads = chunk_loads(z, g, 0, own, sems)
    for cp in loads:
        cp.start()
    (r, before), (l, after) = decode(right), decode(left)
    for cp in loads:
        cp.wait()
    out[...] = (own[...] + r + l) * -SCALE
    loss[0, 0] = jnp.sum(kl[0:1, :] + before + after)


def end_call(z, g, kl, right, left):
    return call(
        end_body,
        (1,),
        [pl.BlockSpec(memory_space=pl.ANY), whole((8, LANES)), whole(MSG), whole(MSG)],
        [whole((CENT, CHUNK)), pl.BlockSpec(memory_space=pltpu.SMEM)],
        [shaped((CENT, CHUNK)), shaped((1, 1))],
        [pltpu.VMEM((CENT, CHUNK), F32), pltpu.SemaphoreType.DMA((PIECES,))],
        prefetch=1,
        vmem=10,
        flops=4 * CENT * CHUNK * 20,
        nbytes=4 << 20,
    )(z, in_hbm(g), kl, right, left)


def point_body(cent, hi, lo, csum, zt, *refs):
    out = refs[-1]
    c = cent[...]
    dims = (((0,), (0,)), ((), ()))
    g = lax.dot_general(c, hi[...], dims, preferred_element_type=F32)
    g = g + lax.dot_general(c, lo[...], dims, preferred_element_type=F32)
    total = jnp.sum(csum[...], axis=0, keepdims=True)
    v = total * zt[...].astype(F32) - g
    expo = exponent(v)
    for k in range(TILE // BLOCK):
        out[k, :, :ROWS] = code(v[k * BLOCK : (k + 1) * BLOCK, :], expo)
        out[k, :, ROWS:] = jnp.broadcast_to(expo, (BLOCK, LANES)).astype(BF16)


def point_call(half, centroids, hi, lo, csum, zt, msgs=None):
    block = (TILE // BLOCK, BLOCK, ROWS + LANES)
    steps = D // TILE // 2
    shape = (NCENT, BLOCK, ROWS + LANES)
    return pl.pallas_call(
        point_body,
        grid=(steps,),
        in_specs=[
            pl.BlockSpec((CENT, TILE), lambda s: (0, s + half * steps)),
            whole((CENT, ROWS)),
            whole((CENT, ROWS)),
            whole((8, ROWS)),
            pl.BlockSpec((TILE, ROWS), lambda s: (s + half * steps, 0)),
        ]
        + ([] if msgs is None else [pl.BlockSpec(memory_space=pl.ANY)]),
        out_specs=pl.BlockSpec(block, lambda s: (s + half * steps, 0, 0)),
        out_shape=pltpu.HBM(shape, BF16),
        input_output_aliases={} if msgs is None else {5: 0},
        compiler_params=pltpu.CompilerParams(
            dimension_semantics=("arbitrary",), vmem_limit_bytes=18 << 20
        ),
        cost_estimate=pl.CostEstimate(flops=2 * CENT * ROWS * D, bytes_accessed=9 << 20, transcendentals=0),
    )(in_hbm(centroids), hi, lo, csum, in_hbm(zt), *([] if msgs is None else [msgs]))


def point_sum_body(msgs, out):
    total = jnp.zeros(out.shape, F32)
    for k in range(NCENT):
        total = total + uncode(msgs[k, :, :ROWS], msgs[k, 0:1, ROWS : ROWS + 1].astype(F32))
    out[...] = total * SCALE


def point_sum_call(msgs):
    return call(
        point_sum_body,
        (1,),
        [whole(msgs.shape)],
        whole((BLOCK, ROWS)),
        shaped((BLOCK, ROWS)),
        vmem=10,
        flops=D * ROWS * 20,
        nbytes=3 << 20,
    )(msgs)


def gather_points(v):
    def stage(v, shifts):
        return jnp.stack([v] + [lax.ppermute(v, "cent", cent_shift(*d)) for d in shifts])

    v = stage(v, [(0, k, 0) for k in (1, 2, 3)])
    v = stage(v, [(k, 0, 0) for k in (1, 2, 3)])
    return v, lax.ppermute(v, "cent", cent_shift(0, 0, 1))


def per_device(points, centroids):
    me = lax.axis_index("cent")
    x, y, c = me // (NY * NC), (me // NC) % NY, me % NC
    at = jnp.stack([x, y, c]).astype(jnp.int32)
    zi = lax.axis_index("pts").astype(jnp.int32)
    z = zi[None]
    mine, other = gather_points(points.T)
    kern, norm, zt, zn = kern_call(at, mine, other, centroids)
    norms = lax.all_to_all(norm, "cent", 0, 0)
    freq, inv = freq_call(norms, kern)
    freqs = lax.all_to_all(freq, "pts", 0, 0)
    den = denom_call(freqs, inv, kern)
    dens = lax.all_to_all(den, "cent", 0, 0)
    hi, lo, csum, kl, g, ra, la = coef_call(z, dens, freqs, inv, kern, centroids, zn)

    def send(right, left):
        return lax.ppermute(right, "pts", z_shift(1)), lax.ppermute(left, "pts", z_shift(-1))

    got = send(ra, la)
    pmsgs = point_call(0, centroids, hi, lo, csum, zt)
    pmsgs, right, left = lax.optimization_barrier((pmsgs, *got))
    msgs = hop_call(z, g, kl, 3, (right, left))
    pmsgs, right, left = lax.optimization_barrier((pmsgs, *msgs))
    got = send(right, left)
    pmsgs = point_call(1, centroids, hi, lo, csum, zt, pmsgs)
    pmsgs, right, left = lax.optimization_barrier((pmsgs, *got))
    got = send(*hop_call(z, g, kl, 2, (right, left)))
    got = send(*hop_call(z, g, kl, 1, got))
    points_t = point_sum_call(lax.all_to_all(pmsgs, "cent", 0, 0))
    points_t, right, left = lax.optimization_barrier((points_t, *got))
    grad_centroids, loss = end_call(z, g, kl, right, left)
    grad_points = points_t.T
    return (grad_points, grad_centroids, loss[0, 0])


def solution(mesh):
    in_specs = (P("pts", "cent"), P("cent", None))
    out_specs = (P("pts", "cent"), P("cent", "pts"), P())
    return jax.shard_map(per_device, mesh=mesh, in_specs=in_specs, out_specs=out_specs, check_vma=False)
```

```python
import functools

import jax
import jax.numpy as jnp
from jax import lax
from jax.experimental import pallas as pl
from jax.experimental.pallas import tpu as pltpu
from jax.sharding import PartitionSpec as P

NX, NY, NC, NZ = 4, 4, 2, 8
NCENT = NX * NY * NC
D = 1024
ROWS = 1024
CENT = 2048
TOTAL = ROWS * NZ
SCALE = 2.0 * CENT * NCENT / TOTAL
CHUNK = D // NZ
HALF = CENT // 2
PAD = 16
TILE = 256
STEPS = CENT // TILE
WIDE = 512
SLAB = 256
WSTEPS = CENT // WIDE
BLOCK = D // NCENT
LANES = 128
F32 = jnp.float32
BF16 = jnp.bfloat16
POWER, WIDTH, SHIFT = 31.0, 255.0, 125.0


def cent_id(x, y, c):
    return (x * NY + y) * NC + c


def cent_shift(dx, dy, dc):
    pairs = []
    for x in range(NX):
        for y in range(NY):
            for c in range(NC):
                pairs.append((cent_id(x, y, c), cent_id((x + dx) % NX, (y + dy) % NY, c ^ dc)))
    return pairs


def z_shift(k):
    return [(i, (i + k) % NZ) for i in range(NZ)]


def dot(a, b):
    return jnp.dot(a, b, preferred_element_type=F32)


def as_row(tile):
    return jnp.concatenate([tile[k : k + 1, :] for k in range(tile.shape[0])], axis=1)


def store_tile(ref, row, lead, first):
    for k in range(row.shape[1] // LANES):
        piece = row[:, k * LANES : (k + 1) * LANES]
        ref[:, first + k, :] = jnp.broadcast_to(piece, (lead, LANES))


def column_blocks(tile, first, count):
    cols = []
    for k in range(count):
        row = tile[first + k : first + k + 1, :]
        cols.append(jnp.transpose(jnp.broadcast_to(row, (LANES, LANES))))
    return jnp.concatenate(cols, axis=0)


def lane_wide(col, width):
    return jnp.concatenate([col] * (width // LANES), axis=1)


def lane_fold(v):
    return functools.reduce(jnp.add, [v[:, k * LANES : (k + 1) * LANES] for k in range(v.shape[1] // LANES)])


def call(body, grid, in_specs, out_specs, out_shape, scratch=(), prefetch=0, vmem=8, flops=0, nbytes=0):
    return pl.pallas_call(
        body,
        grid_spec=pltpu.PrefetchScalarGridSpec(
            num_scalar_prefetch=prefetch,
            grid=grid,
            in_specs=in_specs,
            out_specs=out_specs,
            scratch_shapes=list(scratch),
        ),
        out_shape=out_shape,
        compiler_params=pltpu.CompilerParams(
            dimension_semantics=("arbitrary",) * len(grid), vmem_limit_bytes=vmem << 20
        ),
        cost_estimate=pl.CostEstimate(flops=flops, bytes_accessed=nbytes, transcendentals=0),
    )


def in_hbm(v):
    return pltpu.with_memory_space_constraint(v, pltpu.HBM)


def whole(shape):
    return pl.BlockSpec(shape, lambda *_: (0,) * len(shape))


def shaped(shape, dtype=F32):
    return jax.ShapeDtypeStruct(shape, dtype)


def kern_body(at, mine, other, cent, kern, norm, zt_out, zn_out, zt, zn, zsq, acc, sems, osems):
    step = pl.program_id(0)
    copies = []
    for cr in range(NC):
        src = (mine, other)[cr]
        for xr in range(NX):
            xx = lax.rem(at[0] + NX - xr, NX)
            cc = lax.rem(at[2] + cr, NC)
            copies.append(pltpu.make_async_copy(src.at[xr], zt.at[xx, :, cc], sems.at[cr * NX + xr]))

    @pl.when(step == 0)
    def _():
        for cp in copies:
            cp.start()

    c = cent[...]
    cf = c.astype(F32)
    msq = jnp.sum(lane_fold(cf * cf), axis=1, keepdims=True)
    part = D // WSTEPS
    outs = [pltpu.make_async_copy(zt, zt_out, osems.at[WSTEPS])]
    for t in range(WSTEPS):
        cols = pl.ds(t * part, part)
        outs.append(pltpu.make_async_copy(zn.at[:, cols], zn_out.at[:, cols], osems.at[t]))

    @pl.when(step == 0)
    def _():
        for cp in copies:
            cp.wait()
        outs[0].start()
        total = jnp.zeros((8, ROWS), F32)
        for k in range(D // LANES):
            pair = slice(k % 2 * 2, k % 2 * 2 + 2)
            v = zt[k // 2, pair].reshape(LANES, ROWS).astype(F32)
            v = v * v
            total = total + jnp.sum(v.reshape(LANES // 8, 8, ROWS), axis=0)
        zsq[...] = 1.0 + jnp.sum(total, axis=0, keepdims=True)
        acc[...] = jnp.zeros_like(acc)

    for k in range(ROWS // SLAB):
        cols = slice(k * SLAB, (k + 1) * SLAB)
        dots = dot(c, zt[:, :, :, :, cols].reshape(D, SLAB))
        v = 1.0 / ((zsq[:, cols] + msq) - 2.0 * dots)
        kern[:, cols] = v
        acc[:, cols] += jnp.sum(v.reshape(WIDE // 8, 8, SLAB), axis=0)
    for t in range(WSTEPS):

        @pl.when(step == t)
        def _(t=t):
            zn[:, t * part : (t + 1) * part] = jnp.transpose(zt[t].reshape(part, ROWS))
            outs[1 + t].start()

    @pl.when(step == WSTEPS - 1)
    def _():
        store_tile(norm, jnp.sum(acc[...], axis=0, keepdims=True), NCENT, 0)
        for cp in outs:
            cp.wait()


def kern_call(at, mine, other, centroids):
    hbm = pl.BlockSpec(memory_space=pl.ANY)
    return call(
        kern_body,
        (WSTEPS,),
        [hbm, hbm, pl.BlockSpec((WIDE, D), lambda s, *_: (s, 0))],
        [pl.BlockSpec((WIDE, ROWS), lambda s, *_: (s, 0)), whole((NCENT, 8, LANES)), hbm, hbm],
        [
            shaped((CENT, ROWS)),
            shaped((NCENT, 8, LANES)),
            pltpu.HBM((NX, NY, NC, BLOCK, ROWS), BF16),
            pltpu.HBM((ROWS, D), BF16),
        ],
        [
            pltpu.VMEM((NX, NY, NC, BLOCK, ROWS), BF16),
            pltpu.VMEM((ROWS, D), BF16),
            pltpu.VMEM((1, ROWS), F32),
            pltpu.VMEM((8, ROWS), F32),
            pltpu.SemaphoreType.DMA((NC * NX,)),
            pltpu.SemaphoreType.DMA((WSTEPS + 1,)),
        ],
        prefetch=1,
        vmem=18,
        flops=2 * CENT * ROWS * D,
        nbytes=20 << 20,
    )(at, mine, other, in_hbm(centroids))


def freq_body(norms, kern, freq, inv, row):
    step = pl.program_id(0)

    @pl.when(step == 0)
    def _():
        tile = 1.0 / jnp.sum(norms[...], axis=0)
        inv[...] = tile
        row[...] = as_row(tile)

    part = lane_fold(kern[...] * row[...])
    for k in range(TILE // LANES):
        block = jnp.transpose(part[k * LANES : (k + 1) * LANES, :])
        line = jnp.sum(block, axis=0, keepdims=True)
        freq[:, pl.ds(step * (TILE // LANES) + k, 1), :] = jnp.broadcast_to(line[None], (NZ, 1, LANES))


def freq_call(norms, kern):
    return call(
        freq_body,
        (STEPS,),
        [whole((NCENT, 8, LANES)), pl.BlockSpec((TILE, ROWS), lambda s: (s, 0))],
        [whole((NZ, CENT // LANES, LANES)), whole((8, LANES))],
        [shaped((NZ, CENT // LANES, LANES)), shaped((8, LANES))],
        [pltpu.VMEM((1, ROWS), F32)],
        vmem=6,
        flops=CENT * ROWS * 2,
        nbytes=8 << 20,
    )(norms, kern)


def frequency_columns(rf, step):
    tile = rf[pl.ds(pl.multiple_of(step * (TILE // LANES), TILE // LANES), TILE // LANES), :]
    return lane_wide(column_blocks(tile, 0, TILE // LANES), ROWS)


def denom_body(freqs, inv, kern, out, rf, row, dsum, csum):
    step = pl.program_id(0)

    @pl.when(step == 0)
    def _():
        rf[...] = 1.0 / jnp.sum(freqs[...], axis=0)
        row[...] = as_row(inv[...])
        dsum[...] = jnp.zeros_like(dsum)
        csum[...] = jnp.zeros_like(csum)

    soft = kern[...] * row[...]
    ratio = soft * frequency_columns(rf, step)
    sharp = soft * ratio
    dsum[...] += jnp.sum(sharp.reshape(TILE // 8, 8, ROWS), axis=0)
    csum[...] += jnp.sum((sharp * jnp.log(ratio * float(TOTAL))).reshape(TILE // 8, 8, ROWS), axis=0)

    @pl.when(step == STEPS - 1)
    def _():
        store_tile(out, jnp.sum(dsum[...], axis=0, keepdims=True), NCENT, 0)
        store_tile(out, jnp.sum(csum[...], axis=0, keepdims=True), NCENT, 8)


def denom_call(freqs, inv, kern):
    return call(
        denom_body,
        (STEPS,),
        [
            whole((NZ, CENT // LANES, LANES)),
            whole((8, LANES)),
            pl.BlockSpec((TILE, ROWS), lambda s: (s, 0)),
        ],
        whole((NCENT, 16, LANES)),
        shaped((NCENT, 16, LANES)),
        [
            pltpu.VMEM((CENT // LANES, LANES), F32),
            pltpu.VMEM((1, ROWS), F32),
            pltpu.VMEM((8, ROWS), F32),
            pltpu.VMEM((8, ROWS), F32),
        ],
        vmem=8,
        flops=CENT * ROWS * 6,
        nbytes=8 << 20,
    )(freqs, inv, kern)


def exponent(v):
    size = jnp.abs(v)
    top = jnp.maximum(jnp.max(jnp.max(size, axis=0, keepdims=True), axis=1, keepdims=True), 1e-30)
    return jnp.ceil(jnp.log2(top))


def code(v, expo):
    unit = jnp.minimum(jnp.abs(v) * jnp.exp2(-expo), 1.0)
    c = jnp.exp2(POWER * jnp.log2(1.0 + WIDTH * unit) - SHIFT)
    return jnp.where(v < 0.0, -c, c).astype(BF16)


def uncode(c, expo):
    c = c.astype(F32)
    unit = (jnp.exp2((jnp.log2(jnp.abs(c)) + SHIFT) * (1.0 / POWER)) - 1.0) * (1.0 / WIDTH)
    unit = unit * jnp.exp2(expo)
    return jnp.where(c < 0.0, -unit, unit)


def encode(v, slots, msg):
    rows = v.shape[0]
    expo = exponent(v)
    msg[:rows, :] = code(v, expo)
    high = slots.astype(BF16).astype(F32)
    mid = (slots - high).astype(BF16).astype(F32)
    low = slots - high - mid
    tail = [jnp.broadcast_to(expo, (1, v.shape[1])), high, mid, low, jnp.zeros((PAD - 4, v.shape[1]), F32)]
    msg[rows:, :] = jnp.concatenate(tail, axis=0).astype(BF16)


def decode(msg):
    rows = msg.shape[0] - PAD
    tail = msg[rows:, :].astype(F32)
    return uncode(msg[:rows, :], tail[0:1, :]), (tail[1:2, :] + tail[2:3, :]) + tail[3:4, :]


MSG = (CENT + PAD, CHUNK)
FIRST = (HALF + PAD, CHUNK)


def coef_body(z, dens, freqs, inv, kern, cent, zn_hbm, hi, lo, csum, kl, g, right, left, rf, row, rden, first, zn, sem):
    step = pl.program_id(0)
    rows = [pl.ds(q * (ROWS // 4), ROWS // 4) for q in range(4)]
    loads = [pltpu.make_async_copy(zn_hbm.at[r], zn.at[r], sem.at[q]) for q, r in enumerate(rows)]

    @pl.when(step == 0)
    def _():
        for cp in loads:
            cp.start()
        rf[...] = 1.0 / jnp.sum(freqs[...], axis=0)
        row[...] = as_row(inv[...])
        both = jnp.sum(dens[...], axis=0)
        rtile = 1.0 / both[:8]
        rden[...] = as_row(rtile)
        part = both[8:] * rtile - jnp.log(both[:8] * float(TOTAL))
        part = jnp.sum(jnp.sum(part, axis=0, keepdims=True), axis=1, keepdims=True) * (1.0 / TOTAL)
        lane = lax.broadcasted_iota(jnp.int32, kl.shape, 1)
        kl[...] = jnp.where(lane == z[0], jnp.broadcast_to(part, kl.shape), 0.0)
        csum[...] = jnp.zeros_like(csum)

    far = lax.rem(z[0] + NZ // 2, NZ)
    total = jnp.zeros((8, ROWS), F32)
    for sub in range(WIDE // TILE):
        at = slice(sub * TILE, (sub + 1) * TILE)
        k = kern[at, :]
        soft = k * row[...]
        fc = frequency_columns(rf, step * (WIDE // TILE) + sub)
        coef = k * (soft * soft * fc * rden[...] - soft)
        h = coef.astype(BF16)
        l = (coef - h.astype(F32)).astype(BF16)
        hi[at, :] = h
        lo[at, :] = l
        total = total + jnp.sum(coef.reshape(TILE // 8, 8, ROWS), axis=0)
        e = jnp.sum(lane_fold(coef), axis=1, keepdims=True)
        both = jnp.concatenate([h, l], axis=0)
        if sub == 0:

            @pl.when(step == 0)
            def _():
                for cp in loads:
                    cp.wait()

        for n in range(D // SLAB):
            cols = slice(n * SLAB, (n + 1) * SLAB)
            r = dot(both, zn[:, cols])
            r = r[:TILE] + r[TILE:] - e * cent[at, cols].astype(F32)
            for o in range(SLAB // CHUNK):
                g[n * (SLAB // CHUNK) + o, at, :] = r[:, o * CHUNK : (o + 1) * CHUNK]
    csum[...] += total
    first[pl.ds(pl.multiple_of(step * WIDE, WIDE), WIDE), :] = g[pl.ds(far, 1)][0]

    @pl.when(step == WSTEPS - 1)
    def _():
        encode(first[:HALF, :], kl[0:1, :], right)
        encode(first[HALF:, :], jnp.zeros((1, LANES), F32), left)


def coef_call(z, dens, freqs, inv, kern, centroids, zn):
    tiles = pl.BlockSpec((WIDE, ROWS), lambda s, z: (s, 0))
    return call(
        coef_body,
        (WSTEPS,),
        [
            whole((NCENT, 16, LANES)),
            whole((NZ, CENT // LANES, LANES)),
            whole((8, LANES)),
            tiles,
            pl.BlockSpec((WIDE, D), lambda s, z: (s, 0)),
            pl.BlockSpec(memory_space=pl.ANY),
        ],
        [
            tiles,
            tiles,
            whole((8, ROWS)),
            whole((8, LANES)),
            pl.BlockSpec((NZ, WIDE, CHUNK), lambda s, z: (0, s, 0)),
            whole(FIRST),
            whole(FIRST),
        ],
        [
            shaped((CENT, ROWS), BF16),
            shaped((CENT, ROWS), BF16),
            shaped((8, ROWS)),
            shaped((8, LANES)),
            pltpu.HBM((NZ, CENT, CHUNK), F32),
            shaped(FIRST, BF16),
            shaped(FIRST, BF16),
        ],
        [
            pltpu.VMEM((CENT // LANES, LANES), F32),
            pltpu.VMEM((1, ROWS), F32),
            pltpu.VMEM((1, ROWS), F32),
            pltpu.VMEM((CENT, CHUNK), F32),
            pltpu.VMEM((ROWS, D), BF16),
            pltpu.SemaphoreType.DMA((4,)),
        ],
        prefetch=1,
        vmem=18,
        flops=4 * CENT * ROWS * D,
        nbytes=30 << 20,
    )(z, dens, freqs, inv, in_hbm(kern), in_hbm(centroids), zn)


PIECES = 4


def chunk_loads(z, g, k, part, sems):
    chunk = lax.rem(z[0] + k + NZ, NZ)
    rows = [pl.ds(q * (CENT // PIECES), CENT // PIECES) for q in range(PIECES)]
    return [pltpu.make_async_copy(g.at[chunk, r], part.at[r], sems.at[q]) for q, r in enumerate(rows)]


def hop_body(k, z, g, kl, got_right, got_left, right, left, ahead, behind, sems):
    loads = [chunk_loads(z, g, (k, -k)[i], (ahead, behind)[i], sems.at[i]) for i in range(2)]
    for cp in loads[0] + loads[1]:
        cp.start()
    sums = [decode(got_right), decode(got_left)]
    for cp in loads[0] + loads[1]:
        cp.wait()
    for (v, slots), msg, part, first in zip(sums, (right, left), (ahead, behind), (0, HALF)):
        if k == NZ // 2 - 1:
            own = part[first : first + HALF, :] + v
            rest = part[HALF - first : CENT - first, :]
            full = jnp.concatenate([own, rest] if first == 0 else [rest, own], axis=0)
        else:
            full = part[...] + v
        encode(full, slots + kl[0:1, :], msg)


def hop_call(z, g, kl, k, got):
    return call(
        functools.partial(hop_body, k),
        (1,),
        [pl.BlockSpec(memory_space=pl.ANY), whole((8, LANES)), whole(got[0].shape), whole(got[1].shape)],
        [whole(MSG), whole(MSG)],
        [shaped(MSG, BF16)] * 2,
        [
            pltpu.VMEM((CENT, CHUNK), F32),
            pltpu.VMEM((CENT, CHUNK), F32),
            pltpu.SemaphoreType.DMA((2, PIECES)),
        ],
        prefetch=1,
        vmem=14,
        flops=4 * CENT * CHUNK * 40,
        nbytes=3 << 20,
    )(z, in_hbm(g), kl, *got)


def end_body(z, g, kl, right, left, out, loss, own, sems):
    loads = chunk_loads(z, g, 0, own, sems)
    for cp in loads:
        cp.start()
    (r, before), (l, after) = decode(right), decode(left)
    for cp in loads:
        cp.wait()
    out[...] = (own[...] + r + l) * -SCALE
    loss[0, 0] = jnp.sum(kl[0:1, :] + before + after)


def end_call(z, g, kl, right, left):
    return call(
        end_body,
        (1,),
        [pl.BlockSpec(memory_space=pl.ANY), whole((8, LANES)), whole(MSG), whole(MSG)],
        [whole((CENT, CHUNK)), pl.BlockSpec(memory_space=pltpu.SMEM)],
        [shaped((CENT, CHUNK)), shaped((1, 1))],
        [pltpu.VMEM((CENT, CHUNK), F32), pltpu.SemaphoreType.DMA((PIECES,))],
        prefetch=1,
        vmem=10,
        flops=4 * CENT * CHUNK * 20,
        nbytes=4 << 20,
    )(z, in_hbm(g), kl, right, left)


def point_body(cent, hi, lo, csum, zt, *refs):
    out = refs[-1]
    c = cent[...]
    dims = (((0,), (0,)), ((), ()))
    g = lax.dot_general(c, hi[...], dims, preferred_element_type=F32)
    g = g + lax.dot_general(c, lo[...], dims, preferred_element_type=F32)
    total = jnp.sum(csum[...], axis=0, keepdims=True)
    v = total * zt[...].astype(F32) - g
    expo = exponent(v)
    for k in range(TILE // BLOCK):
        out[k, :, :ROWS] = code(v[k * BLOCK : (k + 1) * BLOCK, :], expo)
        out[k, :, ROWS:] = jnp.broadcast_to(expo, (BLOCK, LANES)).astype(BF16)


def point_call(first, steps, centroids, hi, lo, csum, zt, msgs=None):
    block = (TILE // BLOCK, BLOCK, ROWS + LANES)
    shape = (NCENT, BLOCK, ROWS + LANES)
    return pl.pallas_call(
        point_body,
        grid=(steps,),
        in_specs=[
            pl.BlockSpec((CENT, TILE), lambda s: (0, s + first)),
            whole((CENT, ROWS)),
            whole((CENT, ROWS)),
            whole((8, ROWS)),
            pl.BlockSpec((TILE, ROWS), lambda s: (s + first, 0)),
        ]
        + ([] if msgs is None else [pl.BlockSpec(memory_space=pl.ANY)]),
        out_specs=pl.BlockSpec(block, lambda s: (s + first, 0, 0)),
        out_shape=pltpu.HBM(shape, BF16),
        input_output_aliases={} if msgs is None else {5: 0},
        compiler_params=pltpu.CompilerParams(
            dimension_semantics=("arbitrary",), vmem_limit_bytes=18 << 20
        ),
        cost_estimate=pl.CostEstimate(flops=CENT * ROWS * D * steps, bytes_accessed=9 << 20, transcendentals=0),
    )(in_hbm(centroids), hi, lo, csum, in_hbm(zt), *([] if msgs is None else [msgs]))


def point_sum_body(msgs, out):
    total = jnp.zeros(out.shape, F32)
    for k in range(NCENT):
        total = total + uncode(msgs[k, :, :ROWS], msgs[k, 0:1, ROWS : ROWS + 1].astype(F32))
    out[...] = total * SCALE


def point_sum_call(msgs):
    return call(
        point_sum_body,
        (1,),
        [whole(msgs.shape)],
        whole((BLOCK, ROWS)),
        shaped((BLOCK, ROWS)),
        vmem=10,
        flops=D * ROWS * 20,
        nbytes=3 << 20,
    )(msgs)


def order_body(at, *refs):
    for k in range(NY):
        refs[-1][pl.ds(lax.rem(at[1] + NY - k, NY), 1)] = refs[k][...][None]


def order_call(at, blocks):
    return call(
        order_body,
        (1,),
        [whole((BLOCK, ROWS))] * NY,
        whole((NY, BLOCK, ROWS)),
        shaped((NY, BLOCK, ROWS), BF16),
        prefetch=1,
        nbytes=1 << 19,
    )(at, *blocks)


def gather_points(at, v):
    def stage(v, shifts):
        return [v] + [lax.ppermute(v, "cent", cent_shift(*d)) for d in shifts]

    v = order_call(at, stage(v, [(0, k, 0) for k in (1, 2, 3)]))
    v0, v1, v3, v2 = stage(v, [(k, 0, 0) for k in (1, 3, 2)])
    v = jnp.stack([v0, v1, v2, v3])
    return v, lax.ppermute(v, "cent", cent_shift(0, 0, 1))


def per_device(points, centroids):
    me = lax.axis_index("cent")
    x, y, c = me // (NY * NC), (me // NC) % NY, me % NC
    at = jnp.stack([x, y, c]).astype(jnp.int32)
    zi = lax.axis_index("pts").astype(jnp.int32)
    z = zi[None]
    mine, other = gather_points(at, points.T)
    kern, norm, zt, zn = kern_call(at, mine, other, centroids)
    zt = zt.reshape(D, ROWS)
    norms = lax.all_to_all(norm, "cent", 0, 0)
    freq, inv = freq_call(norms, kern)
    freqs = lax.all_to_all(freq, "pts", 0, 0)
    den = denom_call(freqs, inv, kern)
    dens = lax.all_to_all(den, "cent", 0, 0)
    hi, lo, csum, kl, g, ra, la = coef_call(z, dens, freqs, inv, kern, centroids, zn)

    def send(right, left):
        return lax.ppermute(right, "pts", z_shift(1)), lax.ppermute(left, "pts", z_shift(-1))

    got = send(ra, la)
    pmsgs = point_call(0, 1, centroids, hi, lo, csum, zt)
    pmsgs, right, left = lax.optimization_barrier((pmsgs, *got))
    msgs = hop_call(z, g, kl, 3, (right, left))
    pmsgs, right, left = lax.optimization_barrier((pmsgs, *msgs))
    got = send(right, left)
    pmsgs = point_call(1, D // TILE - 1, centroids, hi, lo, csum, zt, pmsgs)
    pmsgs, right, left = lax.optimization_barrier((pmsgs, *got))
    got = send(*hop_call(z, g, kl, 2, (right, left)))
    got = send(*hop_call(z, g, kl, 1, got))
    points_t = point_sum_call(lax.all_to_all(pmsgs, "cent", 0, 0))
    points_t, right, left = lax.optimization_barrier((points_t, *got))
    grad_centroids, loss = end_call(z, g, kl, right, left)
    grad_points = points_t.T
    return (grad_points, grad_centroids, loss[0, 0])


def solution(mesh):
    in_specs = (P("pts", "cent"), P("cent", None))
    out_specs = (P("pts", "cent"), P("cent", "pts"), P())
    return jax.shard_map(per_device, mesh=mesh, in_specs=in_specs, out_specs=out_specs, check_vma=False)
```

```python
import functools

import jax
import jax.numpy as jnp
from jax import lax
from jax.experimental import pallas as pl
from jax.experimental.pallas import tpu as pltpu
from jax.sharding import PartitionSpec as P

NX, NY, NC, NZ = 4, 4, 2, 8
NCENT = NX * NY * NC
D = 1024
ROWS = 1024
CENT = 2048
TOTAL = ROWS * NZ
SCALE = 2.0 * CENT * NCENT / TOTAL
CHUNK = D // NZ
HALF = CENT // 2
PAD = 16
TILE = 256
STEPS = CENT // TILE
WIDE = 512
KERN = 1024
SLAB = 256
WSTEPS = CENT // WIDE
BLOCK = D // NCENT
LANES = 128
F32 = jnp.float32
BF16 = jnp.bfloat16
POWER, WIDTH, SHIFT = 31.0, 255.0, 125.0


def cent_id(x, y, c):
    return (x * NY + y) * NC + c


def cent_shift(dx, dy, dc):
    pairs = []
    for x in range(NX):
        for y in range(NY):
            for c in range(NC):
                pairs.append((cent_id(x, y, c), cent_id((x + dx) % NX, (y + dy) % NY, c ^ dc)))
    return pairs


def z_shift(k):
    return [(i, (i + k) % NZ) for i in range(NZ)]


def dot(a, b):
    return jnp.dot(a, b, preferred_element_type=F32)


def as_row(tile):
    return jnp.concatenate([tile[k : k + 1, :] for k in range(tile.shape[0])], axis=1)


def store_tile(ref, row, lead, first):
    for k in range(row.shape[1] // LANES):
        piece = row[:, k * LANES : (k + 1) * LANES]
        ref[:, first + k, :] = jnp.broadcast_to(piece, (lead, LANES))


def column_blocks(tile, first, count):
    cols = []
    for k in range(count):
        row = tile[first + k : first + k + 1, :]
        cols.append(jnp.transpose(jnp.broadcast_to(row, (LANES, LANES))))
    return jnp.concatenate(cols, axis=0)


def lane_wide(col, width):
    return jnp.concatenate([col] * (width // LANES), axis=1)


def lane_fold(v):
    return functools.reduce(jnp.add, [v[:, k * LANES : (k + 1) * LANES] for k in range(v.shape[1] // LANES)])


def call(body, grid, in_specs, out_specs, out_shape, scratch=(), prefetch=0, vmem=8, flops=0, nbytes=0):
    return pl.pallas_call(
        body,
        grid_spec=pltpu.PrefetchScalarGridSpec(
            num_scalar_prefetch=prefetch,
            grid=grid,
            in_specs=in_specs,
            out_specs=out_specs,
            scratch_shapes=list(scratch),
        ),
        out_shape=out_shape,
        compiler_params=pltpu.CompilerParams(
            dimension_semantics=("arbitrary",) * len(grid), vmem_limit_bytes=vmem << 20
        ),
        cost_estimate=pl.CostEstimate(flops=flops, bytes_accessed=nbytes, transcendentals=0),
    )


def in_hbm(v):
    return pltpu.with_memory_space_constraint(v, pltpu.HBM)


def whole(shape):
    return pl.BlockSpec(shape, lambda *_: (0,) * len(shape))


def shaped(shape, dtype=F32):
    return jax.ShapeDtypeStruct(shape, dtype)


def kern_body(at, mine, other, cent, kern, norm, zt_out, zn_out, zt, zn, zsq, acc, sems, osems):
    step = pl.program_id(0)
    copies = []
    for cr in range(NC):
        src = (mine, other)[cr]
        for xr in range(NX):
            xx = lax.rem(at[0] + NX - xr, NX)
            cc = lax.rem(at[2] + cr, NC)
            copies.append(pltpu.make_async_copy(src.at[xr], zt.at[xx, :, cc], sems.at[cr * NX + xr]))

    @pl.when(step == 0)
    def _():
        for cp in copies:
            cp.start()

    c = cent[...]
    cf = c.astype(F32)
    msq = jnp.sum(lane_fold(cf * cf), axis=1, keepdims=True)
    part = D // (CENT // KERN)
    nx = NX * KERN // CENT
    outs = [pltpu.make_async_copy(zt, zt_out, osems.at[CENT // KERN])]
    for t in range(CENT // KERN):
        cols = pl.ds(t * part, part)
        outs.append(pltpu.make_async_copy(zn.at[:, cols], zn_out.at[:, cols], osems.at[t]))

    @pl.when(step == 0)
    def _():
        for cp in copies:
            cp.wait()
        outs[0].start()
        total = jnp.zeros((8, ROWS), F32)
        for k in range(D // LANES):
            pair = slice(k % 2 * 2, k % 2 * 2 + 2)
            v = zt[k // 2, pair].reshape(LANES, ROWS).astype(F32)
            v = v * v
            total = total + jnp.sum(v.reshape(LANES // 8, 8, ROWS), axis=0)
        zsq[...] = 1.0 + jnp.sum(total, axis=0, keepdims=True)
        acc[...] = jnp.zeros_like(acc)

    for k in range(ROWS // SLAB):
        cols = slice(k * SLAB, (k + 1) * SLAB)
        dots = dot(c, zt[:, :, :, :, cols].reshape(D, SLAB))
        v = 1.0 / ((zsq[:, cols] + msq) - 2.0 * dots)
        kern[:, cols] = v
        acc[:, cols] += jnp.sum(v.reshape(KERN // 8, 8, SLAB), axis=0)
    for t in range(CENT // KERN):

        @pl.when(step == t)
        def _(t=t):
            zn[:, t * part : (t + 1) * part] = jnp.transpose(zt[t * nx : (t + 1) * nx].reshape(part, ROWS))
            outs[1 + t].start()

    @pl.when(step == CENT // KERN - 1)
    def _():
        store_tile(norm, jnp.sum(acc[...], axis=0, keepdims=True), NCENT, 0)
        for cp in outs:
            cp.wait()


def kern_call(at, mine, other, centroids):
    hbm = pl.BlockSpec(memory_space=pl.ANY)
    return call(
        kern_body,
        (CENT // KERN,),
        [hbm, hbm, pl.BlockSpec((KERN, D), lambda s, *_: (s, 0))],
        [pl.BlockSpec((KERN, ROWS), lambda s, *_: (s, 0)), whole((NCENT, 8, LANES)), hbm, hbm],
        [
            shaped((CENT, ROWS)),
            shaped((NCENT, 8, LANES)),
            pltpu.HBM((NX, NY, NC, BLOCK, ROWS), BF16),
            pltpu.HBM((ROWS, D), BF16),
        ],
        [
            pltpu.VMEM((NX, NY, NC, BLOCK, ROWS), BF16),
            pltpu.VMEM((ROWS, D), BF16),
            pltpu.VMEM((1, ROWS), F32),
            pltpu.VMEM((8, ROWS), F32),
            pltpu.SemaphoreType.DMA((NC * NX,)),
            pltpu.SemaphoreType.DMA((CENT // KERN + 1,)),
        ],
        prefetch=1,
        vmem=24,
        flops=2 * CENT * ROWS * D,
        nbytes=20 << 20,
    )(at, mine, other, in_hbm(centroids))


def freq_body(norms, kern, freq, inv, row):
    step = pl.program_id(0)

    @pl.when(step == 0)
    def _():
        tile = 1.0 / jnp.sum(norms[...], axis=0)
        inv[...] = tile
        row[...] = as_row(tile)

    part = lane_fold(kern[...] * row[...])
    for k in range(TILE // LANES):
        block = jnp.transpose(part[k * LANES : (k + 1) * LANES, :])
        line = jnp.sum(block, axis=0, keepdims=True)
        freq[:, pl.ds(step * (TILE // LANES) + k, 1), :] = jnp.broadcast_to(line[None], (NZ, 1, LANES))


def freq_call(norms, kern):
    return call(
        freq_body,
        (STEPS,),
        [whole((NCENT, 8, LANES)), pl.BlockSpec((TILE, ROWS), lambda s: (s, 0))],
        [whole((NZ, CENT // LANES, LANES)), whole((8, LANES))],
        [shaped((NZ, CENT // LANES, LANES)), shaped((8, LANES))],
        [pltpu.VMEM((1, ROWS), F32)],
        vmem=6,
        flops=CENT * ROWS * 2,
        nbytes=8 << 20,
    )(norms, kern)


def frequency_columns(rf, step):
    tile = rf[pl.ds(pl.multiple_of(step * (TILE // LANES), TILE // LANES), TILE // LANES), :]
    return lane_wide(column_blocks(tile, 0, TILE // LANES), ROWS)


def denom_body(freqs, inv, kern, out, rf, row, dsum, csum):
    step = pl.program_id(0)

    @pl.when(step == 0)
    def _():
        rf[...] = 1.0 / jnp.sum(freqs[...], axis=0)
        row[...] = as_row(inv[...])
        dsum[...] = jnp.zeros_like(dsum)
        csum[...] = jnp.zeros_like(csum)

    soft = kern[...] * row[...]
    ratio = soft * frequency_columns(rf, step)
    sharp = soft * ratio
    dsum[...] += jnp.sum(sharp.reshape(TILE // 8, 8, ROWS), axis=0)
    csum[...] += jnp.sum((sharp * jnp.log(ratio * float(TOTAL))).reshape(TILE // 8, 8, ROWS), axis=0)

    @pl.when(step == STEPS - 1)
    def _():
        store_tile(out, jnp.sum(dsum[...], axis=0, keepdims=True), NCENT, 0)
        store_tile(out, jnp.sum(csum[...], axis=0, keepdims=True), NCENT, 8)


def denom_call(freqs, inv, kern):
    return call(
        denom_body,
        (STEPS,),
        [
            whole((NZ, CENT // LANES, LANES)),
            whole((8, LANES)),
            pl.BlockSpec((TILE, ROWS), lambda s: (s, 0)),
        ],
        whole((NCENT, 16, LANES)),
        shaped((NCENT, 16, LANES)),
        [
            pltpu.VMEM((CENT // LANES, LANES), F32),
            pltpu.VMEM((1, ROWS), F32),
            pltpu.VMEM((8, ROWS), F32),
            pltpu.VMEM((8, ROWS), F32),
        ],
        vmem=8,
        flops=CENT * ROWS * 6,
        nbytes=8 << 20,
    )(freqs, inv, kern)


def exponent(v):
    size = jnp.abs(v)
    top = jnp.maximum(jnp.max(jnp.max(size, axis=0, keepdims=True), axis=1, keepdims=True), 1e-30)
    return jnp.ceil(jnp.log2(top))


def code(v, expo):
    unit = jnp.minimum(jnp.abs(v) * jnp.exp2(-expo), 1.0)
    c = jnp.exp2(POWER * jnp.log2(1.0 + WIDTH * unit) - SHIFT)
    return jnp.where(v < 0.0, -c, c).astype(BF16)


def uncode(c, expo):
    c = c.astype(F32)
    unit = (jnp.exp2((jnp.log2(jnp.abs(c)) + SHIFT) * (1.0 / POWER)) - 1.0) * (1.0 / WIDTH)
    unit = unit * jnp.exp2(expo)
    return jnp.where(c < 0.0, -unit, unit)


def encode(v, slots, msg):
    rows = v.shape[0]
    expo = exponent(v)
    msg[:rows, :] = code(v, expo)
    high = slots.astype(BF16).astype(F32)
    mid = (slots - high).astype(BF16).astype(F32)
    low = slots - high - mid
    tail = [jnp.broadcast_to(expo, (1, v.shape[1])), high, mid, low, jnp.zeros((PAD - 4, v.shape[1]), F32)]
    msg[rows:, :] = jnp.concatenate(tail, axis=0).astype(BF16)


def decode(msg):
    rows = msg.shape[0] - PAD
    tail = msg[rows:, :].astype(F32)
    return uncode(msg[:rows, :], tail[0:1, :]), (tail[1:2, :] + tail[2:3, :]) + tail[3:4, :]


MSG = (CENT + PAD, CHUNK)
FIRST = (HALF + PAD, CHUNK)


def coef_body(z, dens, freqs, inv, kern, cent, zn_hbm, hi, lo, csum, kl, g, right, left, rf, row, rden, first, zn, sem):
    step = pl.program_id(0)
    rows = [pl.ds(q * (ROWS // 4), ROWS // 4) for q in range(4)]
    loads = [pltpu.make_async_copy(zn_hbm.at[r], zn.at[r], sem.at[q]) for q, r in enumerate(rows)]

    @pl.when(step == 0)
    def _():
        for cp in loads:
            cp.start()
        rf[...] = 1.0 / jnp.sum(freqs[...], axis=0)
        row[...] = as_row(inv[...])
        both = jnp.sum(dens[...], axis=0)
        rtile = 1.0 / both[:8]
        rden[...] = as_row(rtile)
        part = both[8:] * rtile - jnp.log(both[:8] * float(TOTAL))
        part = jnp.sum(jnp.sum(part, axis=0, keepdims=True), axis=1, keepdims=True) * (1.0 / TOTAL)
        lane = lax.broadcasted_iota(jnp.int32, kl.shape, 1)
        kl[...] = jnp.where(lane == z[0], jnp.broadcast_to(part, kl.shape), 0.0)
        csum[...] = jnp.zeros_like(csum)

    far = lax.rem(z[0] + NZ // 2, NZ)
    total = jnp.zeros((8, ROWS), F32)
    for sub in range(WIDE // TILE):
        at = slice(sub * TILE, (sub + 1) * TILE)
        k = kern[at, :]
        soft = k * row[...]
        fc = frequency_columns(rf, step * (WIDE // TILE) + sub)
        coef = k * (soft * soft * fc * rden[...] - soft)
        h = coef.astype(BF16)
        l = (coef - h.astype(F32)).astype(BF16)
        hi[at, :] = h
        lo[at, :] = l
        total = total + jnp.sum(coef.reshape(TILE // 8, 8, ROWS), axis=0)
        e = jnp.sum(lane_fold(coef), axis=1, keepdims=True)
        both = jnp.concatenate([h, l], axis=0)
        if sub == 0:

            @pl.when(step == 0)
            def _():
                for cp in loads:
                    cp.wait()

        for n in range(D // SLAB):
            cols = slice(n * SLAB, (n + 1) * SLAB)
            r = dot(both, zn[:, cols])
            r = r[:TILE] + r[TILE:] - e * cent[at, cols].astype(F32)
            for o in range(SLAB // CHUNK):
                g[n * (SLAB // CHUNK) + o, at, :] = r[:, o * CHUNK : (o + 1) * CHUNK]
    csum[...] += total
    first[pl.ds(pl.multiple_of(step * WIDE, WIDE), WIDE), :] = g[pl.ds(far, 1)][0]

    @pl.when(step == WSTEPS - 1)
    def _():
        encode(first[:HALF, :], kl[0:1, :], right)
        encode(first[HALF:, :], jnp.zeros((1, LANES), F32), left)


def coef_call(z, dens, freqs, inv, kern, centroids, zn):
    tiles = pl.BlockSpec((WIDE, ROWS), lambda s, z: (s, 0))
    return call(
        coef_body,
        (WSTEPS,),
        [
            whole((NCENT, 16, LANES)),
            whole((NZ, CENT // LANES, LANES)),
            whole((8, LANES)),
            tiles,
            pl.BlockSpec((WIDE, D), lambda s, z: (s, 0)),
            pl.BlockSpec(memory_space=pl.ANY),
        ],
        [
            tiles,
            tiles,
            whole((8, ROWS)),
            whole((8, LANES)),
            pl.BlockSpec((NZ, WIDE, CHUNK), lambda s, z: (0, s, 0)),
            whole(FIRST),
            whole(FIRST),
        ],
        [
            shaped((CENT, ROWS), BF16),
            shaped((CENT, ROWS), BF16),
            shaped((8, ROWS)),
            shaped((8, LANES)),
            pltpu.HBM((NZ, CENT, CHUNK), F32),
            shaped(FIRST, BF16),
            shaped(FIRST, BF16),
        ],
        [
            pltpu.VMEM((CENT // LANES, LANES), F32),
            pltpu.VMEM((1, ROWS), F32),
            pltpu.VMEM((1, ROWS), F32),
            pltpu.VMEM((CENT, CHUNK), F32),
            pltpu.VMEM((ROWS, D), BF16),
            pltpu.SemaphoreType.DMA((4,)),
        ],
        prefetch=1,
        vmem=18,
        flops=4 * CENT * ROWS * D,
        nbytes=30 << 20,
    )(z, dens, freqs, inv, in_hbm(kern), in_hbm(centroids), zn)


PIECES = 4


def chunk_loads(z, g, k, part, sems):
    chunk = lax.rem(z[0] + k + NZ, NZ)
    rows = [pl.ds(q * (CENT // PIECES), CENT // PIECES) for q in range(PIECES)]
    return [pltpu.make_async_copy(g.at[chunk, r], part.at[r], sems.at[q]) for q, r in enumerate(rows)]


def hop_body(k, z, g, kl, got_right, got_left, right, left, ahead, behind, sems):
    loads = [chunk_loads(z, g, (k, -k)[i], (ahead, behind)[i], sems.at[i]) for i in range(2)]
    for cp in loads[0] + loads[1]:
        cp.start()
    sums = [decode(got_right), decode(got_left)]
    for cp in loads[0] + loads[1]:
        cp.wait()
    for (v, slots), msg, part, first in zip(sums, (right, left), (ahead, behind), (0, HALF)):
        if k == NZ // 2 - 1:
            own = part[first : first + HALF, :] + v
            rest = part[HALF - first : CENT - first, :]
            full = jnp.concatenate([own, rest] if first == 0 else [rest, own], axis=0)
        else:
            full = part[...] + v
        encode(full, slots + kl[0:1, :], msg)


def hop_call(z, g, kl, k, got):
    return call(
        functools.partial(hop_body, k),
        (1,),
        [pl.BlockSpec(memory_space=pl.ANY), whole((8, LANES)), whole(got[0].shape), whole(got[1].shape)],
        [whole(MSG), whole(MSG)],
        [shaped(MSG, BF16)] * 2,
        [
            pltpu.VMEM((CENT, CHUNK), F32),
            pltpu.VMEM((CENT, CHUNK), F32),
            pltpu.SemaphoreType.DMA((2, PIECES)),
        ],
        prefetch=1,
        vmem=14,
        flops=4 * CENT * CHUNK * 40,
        nbytes=3 << 20,
    )(z, in_hbm(g), kl, *got)


def end_body(z, g, kl, right, left, out, loss, own, sems):
    loads = chunk_loads(z, g, 0, own, sems)
    for cp in loads:
        cp.start()
    (r, before), (l, after) = decode(right), decode(left)
    for cp in loads:
        cp.wait()
    out[...] = (own[...] + r + l) * -SCALE
    loss[0, 0] = jnp.sum(kl[0:1, :] + before + after)


def end_call(z, g, kl, right, left):
    return call(
        end_body,
        (1,),
        [pl.BlockSpec(memory_space=pl.ANY), whole((8, LANES)), whole(MSG), whole(MSG)],
        [whole((CENT, CHUNK)), pl.BlockSpec(memory_space=pltpu.SMEM)],
        [shaped((CENT, CHUNK)), shaped((1, 1))],
        [pltpu.VMEM((CENT, CHUNK), F32), pltpu.SemaphoreType.DMA((PIECES,))],
        prefetch=1,
        vmem=10,
        flops=4 * CENT * CHUNK * 20,
        nbytes=4 << 20,
    )(z, in_hbm(g), kl, right, left)


def point_body(cent, hi, lo, csum, zt, *refs):
    out = refs[-1]
    c = cent[...]
    dims = (((0,), (0,)), ((), ()))
    g = lax.dot_general(c, hi[...], dims, preferred_element_type=F32)
    g = g + lax.dot_general(c, lo[...], dims, preferred_element_type=F32)
    total = jnp.sum(csum[...], axis=0, keepdims=True)
    v = total * zt[...].astype(F32) - g
    expo = exponent(v)
    for k in range(TILE // BLOCK):
        out[k, :, :ROWS] = code(v[k * BLOCK : (k + 1) * BLOCK, :], expo)
        out[k, :, ROWS:] = jnp.broadcast_to(expo, (BLOCK, LANES)).astype(BF16)


def point_call(first, steps, centroids, hi, lo, csum, zt, msgs=None):
    block = (TILE // BLOCK, BLOCK, ROWS + LANES)
    shape = (NCENT, BLOCK, ROWS + LANES)
    return pl.pallas_call(
        point_body,
        grid=(steps,),
        in_specs=[
            pl.BlockSpec((CENT, TILE), lambda s: (0, s + first)),
            whole((CENT, ROWS)),
            whole((CENT, ROWS)),
            whole((8, ROWS)),
            pl.BlockSpec((TILE, ROWS), lambda s: (s + first, 0)),
        ]
        + ([] if msgs is None else [pl.BlockSpec(memory_space=pl.ANY)]),
        out_specs=pl.BlockSpec(block, lambda s: (s + first, 0, 0)),
        out_shape=pltpu.HBM(shape, BF16),
        input_output_aliases={} if msgs is None else {5: 0},
        compiler_params=pltpu.CompilerParams(
            dimension_semantics=("arbitrary",), vmem_limit_bytes=18 << 20
        ),
        cost_estimate=pl.CostEstimate(flops=CENT * ROWS * D * steps, bytes_accessed=9 << 20, transcendentals=0),
    )(in_hbm(centroids), hi, lo, csum, in_hbm(zt), *([] if msgs is None else [msgs]))


def point_sum_body(msgs, out):
    total = jnp.zeros(out.shape, F32)
    for k in range(NCENT):
        total = total + uncode(msgs[k, :, :ROWS], msgs[k, 0:1, ROWS : ROWS + 1].astype(F32))
    out[...] = total * SCALE


def point_sum_call(msgs):
    return call(
        point_sum_body,
        (1,),
        [whole(msgs.shape)],
        whole((BLOCK, ROWS)),
        shaped((BLOCK, ROWS)),
        vmem=10,
        flops=D * ROWS * 20,
        nbytes=3 << 20,
    )(msgs)


def order_body(at, *refs):
    for k in range(NY):
        refs[-1][pl.ds(lax.rem(at[1] + NY - k, NY), 1)] = refs[k][...][None]


def order_call(at, blocks):
    return call(
        order_body,
        (1,),
        [whole((BLOCK, ROWS))] * NY,
        whole((NY, BLOCK, ROWS)),
        shaped((NY, BLOCK, ROWS), BF16),
        prefetch=1,
        nbytes=1 << 19,
    )(at, in_hbm(blocks[0]), *blocks[1:])


def gather_points(at, v):
    def stage(v, shifts):
        return [v] + [lax.ppermute(v, "cent", cent_shift(*d)) for d in shifts]

    v = order_call(at, stage(v, [(0, k, 0) for k in (1, 2, 3)]))
    v0, v1, v3, v2 = stage(v, [(k, 0, 0) for k in (1, 3, 2)])
    v = jnp.stack([v0, v1, v2, v3])
    return v, lax.ppermute(v, "cent", cent_shift(0, 0, 1))


def per_device(points, centroids):
    me = lax.axis_index("cent")
    x, y, c = me // (NY * NC), (me // NC) % NY, me % NC
    at = jnp.stack([x, y, c]).astype(jnp.int32)
    zi = lax.axis_index("pts").astype(jnp.int32)
    z = zi[None]
    mine, other = gather_points(at, points.T)
    kern, norm, zt, zn = kern_call(at, mine, other, centroids)
    zt = zt.reshape(D, ROWS)
    norms = lax.all_to_all(norm, "cent", 0, 0)
    freq, inv = freq_call(norms, kern)
    freqs = lax.all_to_all(freq, "pts", 0, 0)
    den = denom_call(freqs, inv, kern)
    dens = lax.all_to_all(den, "cent", 0, 0)
    hi, lo, csum, kl, g, ra, la = coef_call(z, dens, freqs, inv, kern, centroids, zn)

    def send(right, left):
        return lax.ppermute(right, "pts", z_shift(1)), lax.ppermute(left, "pts", z_shift(-1))

    got = send(ra, la)
    pmsgs = point_call(0, 1, centroids, hi, lo, csum, zt)
    pmsgs, right, left = lax.optimization_barrier((pmsgs, *got))
    msgs = hop_call(z, g, kl, 3, (right, left))
    pmsgs, right, left = lax.optimization_barrier((pmsgs, *msgs))
    got = send(right, left)
    pmsgs = point_call(1, D // TILE - 1, centroids, hi, lo, csum, zt, pmsgs)
    pmsgs, right, left = lax.optimization_barrier((pmsgs, *got))
    got = send(*hop_call(z, g, kl, 2, (right, left)))
    got = send(*hop_call(z, g, kl, 1, got))
    points_t = point_sum_call(lax.all_to_all(pmsgs, "cent", 0, 0))
    points_t, right, left = lax.optimization_barrier((points_t, *got))
    grad_centroids, loss = end_call(z, g, kl, right, left)
    grad_points = points_t.T
    return (grad_points, grad_centroids, loss[0, 0])


def solution(mesh):
    in_specs = (P("pts", "cent"), P("cent", None))
    out_specs = (P("pts", "cent"), P("cent", "pts"), P())
    return jax.shard_map(per_device, mesh=mesh, in_specs=in_specs, out_specs=out_specs, check_vma=False)
```
